256 devices in a mesh: gy: 8 (over z_hi, core), gz: 32 (over y, x, z_lo).
Axes of the slice: x: 4, y: 4, z: 8 (z_hi: 4, z_lo: 2; z = z_hi * 2 + z_lo), core: 2. Of those that a mesh axis runs over, the one named last changes fastest.
Arguments:
- ex: float32 [128, 256, 512], P('gy', 'gz'), may hold values from -6 to 6
- ey: float32 [128, 256, 512], P('gy', 'gz'), may hold values from -6 to 6
- ez: float32 [128, 256, 512], P('gy', 'gz'), may hold values from -6 to 6
- hx: float32 [128, 256, 512], P('gy', 'gz'), may hold values from -6 to 6
- hy: float32 [128, 256, 512], P('gy', 'gz'), may hold values from -6 to 6
- hz: float32 [128, 256, 512], P('gy', 'gz'), may hold values from -6 to 6
- material: int32 [128, 256, 512], P('gy', 'gz'), may hold values from 0 to 15
- eps_table: float32 [16], replicated, may hold values from 1 to 4
- mu_table: float32 [16], replicated, may hold values from 1 to 2
Outputs:
- ex_new: float32 [128, 256, 512], P('gy', 'gz')
- ey_new: float32 [128, 256, 512], P('gy', 'gz')
- ez_new: float32 [128, 256, 512], P('gy', 'gz')
- hx_new: float32 [128, 256, 512], P('gy', 'gz')
- hy_new: float32 [128, 256, 512], P('gy', 'gz')
- hz_new: float32 [128, 256, 512], P('gy', 'gz')
The draws below stay inside these ranges and needn't reach their ends.
Inputs may be any that keep to these rules, and one draw needn't show every extreme that they name: material indexes the two tables.
All inputs are finite; a program needn't handle non-finite values.
Results may differ from the reference program's by a relative error of at most 0.00026.
Values sent between devices are 32-bit elements; how exact they have to be, the bound alone decides.
No kernel may reach another device: no remote copies, remote signals or barrier semaphores. Data moves between devices by JAX's collectives and lax.ppermute only.
A program may use at most 128 MiB of HBM per device.

```python
import math
import jax
import jax.numpy as jnp
from jax import lax

NX = 512
MATERIALS = 16
NY = 128
NZ = 256


def plant(values, key, least, high):
    longest = values.shape.index(max(values.shape))
    spots = []
    for shift in (0, 1):
        where = [jax.random.randint(jax.random.fold_in(key, axis), (), 0, length) for axis, length in enumerate(values.shape)]
        where[longest] = (where[longest] + shift) % values.shape[longest]
        spots.append(tuple(where))
    return values.at[spots[0]].set(least).at[spots[1]].set(high)


def steps_of(rng, shape, pieces, low, top_value):
    def one(position, shards_of):
        draws = jax.random.uniform(jax.random.fold_in(jax.random.fold_in(rng, 6), position), (shards_of,), jnp.float32, low / len(pieces), top_value / len(pieces))
        return jnp.repeat(jnp.exp(draws), shape[position] // shards_of).reshape((-1,) + (1,) * (len(shape) - position - 1))

    factor_of = one(*pieces[0])
    for cut in pieces[1:]:
        factor_of = factor_of * one(*cut)
    return factor_of


def normal_values(stream_key, dims, deviation, bound, shards=(), kind=jnp.bfloat16):
    array = jax.random.normal(stream_key, dims, jnp.float32) * deviation
    if len(shards) > 0:
        array = steps_of(stream_key, dims, shards, -0.22, 0.18) * array
    return jnp.clip(array, min=-bound, max=bound).astype(kind)


def setup_inputs(seed: int = 0) -> dict:
    key_list = jax.random.split(jax.random.key(seed), 10)
    ex = normal_values(key_list[0], (NY, NZ, NX), 1.0, 6.0, ((0, 8), (1, 32)), jnp.float32)
    ey = normal_values(key_list[1], (NY, NZ, NX), 1.0, 6.0, ((0, 8), (1, 32)), jnp.float32)
    ez = normal_values(key_list[2], (NY, NZ, NX), 1.0, 6.0, ((0, 8), (1, 32)), jnp.float32)
    hx = normal_values(key_list[3], (NY, NZ, NX), 1.0, 6.0, ((0, 8), (1, 32)), jnp.float32)
    hy = normal_values(key_list[4], (NY, NZ, NX), 1.0, 6.0, ((0, 8), (1, 32)), jnp.float32)
    hz = normal_values(key_list[5], (NY, NZ, NX), 1.0, 6.0, ((0, 8), (1, 32)), jnp.float32)
    material = plant(jax.random.randint(key_list[6], (NY, NZ, NX), 0, MATERIALS), jax.random.fold_in(key_list[6], 1), 0, MATERIALS - 1).astype(jnp.int32)
    eps_table = jnp.clip(jnp.exp(jax.random.uniform(key_list[7], (MATERIALS,), jnp.float32, math.log(1.0), math.log(4.0))), 1.0, 4.0)
    mu_table = jnp.clip(jnp.exp(jax.random.uniform(key_list[8], (MATERIALS,), jnp.float32, math.log(1.0), math.log(2.0))), 1.0, 2.0)
    return {"ex": ex, "ey": ey, "ez": ez, "hx": hx, "hy": hy, "hz": hz, "material": material, "eps_table": eps_table, "mu_table": mu_table}


courant = 16.0

def shift_prev(field, axis):
    size = field.shape[axis]
    first = jnp.zeros_like(lax.slice_in_dim(field, 0, 1, axis=axis))
    return jnp.concatenate([first, lax.slice_in_dim(field, 0, size - 1, axis=axis)], axis=axis)

def shift_next(field, axis):
    size = field.shape[axis]
    final = jnp.zeros_like(lax.slice_in_dim(field, 0, 1, axis=axis))
    return jnp.concatenate([lax.slice_in_dim(field, 1, size, axis=axis), final], axis=axis)

def back_diff(field, axis):
    return field - shift_prev(field, axis)

def fwd_diff(field, axis):
    return shift_next(field, axis) - field

def band_solve(rhs, coef_e, coef_h):
    zeros = jnp.zeros_like(coef_h[..., :1])
    h_prev = jnp.concatenate([zeros, coef_h[..., :-1]], -1)
    lower = -coef_e * h_prev
    diag = 1.0 + coef_e * (coef_h + h_prev)
    upper = jnp.concatenate([(-coef_e * coef_h)[..., :-1], zeros], -1)
    return lax.linalg.tridiagonal_solve(lower, diag, upper, rhs[..., None])[..., 0]

def line_solve(rhs, coef_e, coef_h, axis):
    moved = band_solve(jnp.moveaxis(rhs, axis, -1), jnp.moveaxis(coef_e, axis, -1), jnp.moveaxis(coef_h, axis, -1))
    return jnp.moveaxis(moved, -1, axis)

def reference(ex, ey, ez, hx, hy, hz, material, eps_table, mu_table):
    coef_e = courant / eps_table[material]
    coef_h = courant / mu_table[material]
    yaxis, zaxis, xaxis = (0, 1, 2)
    hz_t = hz - coef_h * fwd_diff(ey, xaxis)
    ex1 = line_solve(ex + coef_e * (back_diff(hz_t, yaxis) - back_diff(hy, zaxis)), coef_e, coef_h, yaxis)
    dy_ex1 = fwd_diff(ex1, yaxis)
    hz1 = hz_t + coef_h * dy_ex1
    hx_t = hx - coef_h * fwd_diff(ez, yaxis)
    ey1 = line_solve(ey + coef_e * (back_diff(hx_t, zaxis) - back_diff(hz, xaxis)), coef_e, coef_h, zaxis)
    dz_ey1 = fwd_diff(ey1, zaxis)
    hx1 = hx_t + coef_h * dz_ey1
    hy_t = hy - coef_h * fwd_diff(ex, zaxis)
    ez1 = line_solve(ez + coef_e * (back_diff(hy_t, xaxis) - back_diff(hx, yaxis)), coef_e, coef_h, xaxis)
    dx_ez1 = fwd_diff(ez1, xaxis)
    hy1 = hy_t + coef_h * dx_ez1
    hy_u = hy1 + coef_h * dx_ez1
    ex_new = line_solve(ex1 + coef_e * (-back_diff(hy_u, zaxis) + back_diff(hz1, yaxis)), coef_e, coef_h, zaxis)
    hy_new = hy_u - coef_h * fwd_diff(ex_new, zaxis)
    hz_u = hz1 + coef_h * dy_ex1
    ey_new = line_solve(ey1 + coef_e * (-back_diff(hz_u, xaxis) + back_diff(hx1, zaxis)), coef_e, coef_h, xaxis)
    hz_new = hz_u - coef_h * fwd_diff(ey_new, xaxis)
    hx_u = hx1 + coef_h * dz_ey1
    ez_new = line_solve(ez1 + coef_e * (-back_diff(hx_u, yaxis) + back_diff(hy1, xaxis)), coef_e, coef_h, yaxis)
    hx_new = hx_u - coef_h * fwd_diff(ez_new, yaxis)
    return (ex_new, ey_new, ez_new, hx_new, hy_new, hz_new)
```

```python
import functools

import jax
import jax.numpy as jnp
from jax import lax
from jax.experimental import pallas as pl
from jax.experimental.pallas import tpu as pltpu
from jax.sharding import PartitionSpec as P

courant = 16.0
F32 = jnp.float32
NYL, NZL, NX = 16, 8, 512
ROWS = NYL * NZL
LANES = 128
CHUNKS = NX // LANES
RUN = NX // 8

Y_STEPS = ((1, 0), (2, 1), (6, 2))
Z_STEPS = ((1, 0), (2, 1), (6, 2), (8, 3), (24, 4))


def shifted(array, axis, by):
    size = lax.axis_size(axis)
    pairs = [(i, i + by) for i in range(size) if 0 <= i + by < size]
    return lax.ppermute(array, axis, pairs)


def swapped(array, axis, flip):
    size = lax.axis_size(axis)
    return lax.ppermute(array, axis, [(i, i ^ flip) for i in range(size)])


def merge_mat(s1, s2):
    ga1, b1, gc1 = s1
    ga2, b2, gc2 = s2
    ground = ga2 if gc1 is None else gc1 + ga2
    inv = 1.0 / (b1 + b2 + ground)
    p, q = b1 * inv, b2 * inv
    right = q * ground
    return (ga1 + p * ground, p * b2, right if gc2 is None else gc2 + right), (p, q, inv)


def merge_rhs(r1, r2, p, q):
    w = r1[1] + r2[0]
    return (r1[0] + p * w, r2[1] + q * w), w


def tree_mat(lo, hi, leaf, put):
    if hi - lo == 1:
        return leaf(lo)
    mid = (lo + hi) // 2
    left = tree_mat(lo, mid, leaf, put)
    right = tree_mat(mid, hi, leaf, put)
    stamp, coefs = merge_mat(left, right)
    put(mid - 1, coefs)
    return stamp


def tree_rhs(lo, hi, leaf, coef, put):
    if hi - lo == 1:
        return leaf(lo)
    mid = (lo + hi) // 2
    left = tree_rhs(lo, mid, leaf, coef, put)
    right = tree_rhs(mid, hi, leaf, coef, put)
    out, w = merge_rhs(left, right, coef(0, mid - 1), coef(1, mid - 1))
    put(mid - 1, w)
    return out


def tree_down(lo, hi, x_lo, x_hi, coef, source, put):
    if hi - lo == 1:
        put(lo, x_lo, x_hi)
        return
    mid = (lo + hi) // 2
    k = mid - 1
    x_mid = coef(0, k) * x_lo + coef(1, k) * x_hi + coef(2, k) * source(k)
    tree_down(lo, mid, x_lo, x_mid, coef, source, put)
    tree_down(mid, hi, x_mid, x_hi, coef, source, put)


def cut(c):
    return pl.ds(c * LANES, LANES)


def plain(y):
    return pl.ds(y * NZL, NZL)


def yrow(y, c):
    return pl.ds((y * CHUNKS + c) * NZL, NZL)


def zrow(z, c):
    return pl.ds(c * NZL + z, NYL, stride=CHUNKS * NZL)


def wide(ref, y):
    return jnp.concatenate([ref[yrow(y, c), :] for c in range(CHUNKS)], axis=1)


def put_wide(ref, y, value):
    for c in range(CHUNKS):
        ref[yrow(y, c), :] = value[:, c * LANES:(c + 1) * LANES]


def tall(ref, c):
    return jnp.concatenate([ref[yrow(y, c), :] for y in range(NYL)], axis=0)


def next_x(v):
    lane = lax.broadcasted_iota(jnp.int32, v.shape, 1)
    return jnp.where(lane == NX - 1, 0.0, pltpu.roll(v, NX - 1, 1))


def prev_x(v):
    lane = lax.broadcasted_iota(jnp.int32, v.shape, 1)
    return jnp.where(lane == 0, 0.0, pltpu.roll(v, 1, 1))


def bit_of(axis, bit):
    return (lax.axis_index(axis) >> bit) & 1


def rims_kernel(hy, ez, ex, hx, hy_top, ez_first, ex_first, hx_last):
    ez_first[...] = ez[...]
    hx_last[...] = hx[...]
    for y in range(NYL):
        hy_top[y:y + 1, :] = hy[(y + 1) * NZL - 1:(y + 1) * NZL, :]
        ex_first[y:y + 1, :] = ex[y * NZL:y * NZL + 1, :]


def bands_kernel(material, eps, mu, ie, ch, y_mat, z_mat, cy, cz):
    for y in range(NYL):
        for c in range(CHUNKS):
            label = material[plain(y), cut(c)]
            e_val = jnp.full(label.shape, eps[0], F32)
            m_val = jnp.full(label.shape, mu[0], F32)
            for k in range(1, 16):
                hit = label == k
                e_val = jnp.where(hit, eps[k], e_val)
                m_val = jnp.where(hit, mu[k], m_val)
            ie[yrow(y, c), :] = e_val * (1.0 / courant)
            ch[yrow(y, c), :] = courant / m_val
    for c in range(CHUNKS):
        for rows, count, mat, coef in ((yrow, NYL, y_mat, cy), (zrow, NZL, z_mat, cz)):

            def leaf(i):
                return ie[rows(i, c), :], ch[rows(i, c), :], None

            def put(k, coefs):
                for j in range(3):
                    coef[j * (count - 1) + k, :, cut(c)] = coefs[j]

            for j, part in enumerate(tree_mat(0, count, leaf, put)):
                mat[j, :, cut(c)] = part


def up_local(rows, count, c, f_of, g_of, coef, w_out, pay):
    def leaf(i):
        return f_of[rows(i, c), :], g_of[rows(i, c), :]

    def get(j, k):
        return coef[j * (count - 1) + k, :, cut(c)]

    def put(k, w):
        w_out[k, :, cut(c)] = w

    f, g = tree_rhs(0, count, leaf, get, put)
    pay[0, :, cut(c)] = f
    pay[1, :, cut(c)] = g


def first_y_kernel(hz, ey, ex, hy, hy_rim, ie, ch, y_mat, cy, pay, w_out, hz_t, f_s, g_s):
    for y in range(NYL):
        r = plain(y)
        ey_r = ey[r, :]
        ht = hz[r, :] - wide(ch, y) * (next_x(ey_r) - ey_r)
        hy_r = hy[r, :]
        z_of = lax.broadcasted_iota(jnp.int32, hy_r.shape, 0)
        low = jnp.where(z_of == 0, jnp.broadcast_to(hy_rim[y:y + 1, :], hy_r.shape), pltpu.roll(hy_r, 1, 0))
        put_wide(hz_t, y, ht)
        put_wide(f_s, y, wide(ie, y) * ex[r, :] - (hy_r - low) + ht)
        put_wide(g_s, y, -ht)
    for c in range(CHUNKS):
        up_local(yrow, NYL, c, f_s, g_s, cy, w_out, pay)
    pay[2:5] = y_mat[...]


def first_z_kernel(hx, ez, ez_rim, hz, ey, ie, ch, z_mat, cz, pay, w_out, hx_t, f_s, g_s):
    for y in range(NYL):
        r = plain(y)
        up = ez[plain(y + 1), :] if y < NYL - 1 else ez_rim[...]
        ht = hx[r, :] - wide(ch, y) * (up - ez[r, :])
        hz_r = hz[r, :]
        put_wide(hx_t, y, ht)
        put_wide(f_s, y, wide(ie, y) * ey[r, :] - (hz_r - prev_x(hz_r)) + ht)
        put_wide(g_s, y, -ht)
    for c in range(CHUNKS):
        up_local(zrow, NZL, c, f_s, g_s, cz, w_out, pay)
    pay[2:5] = z_mat[...]


def merge_all(lower, upper, pay, save):
    stamp, (p, q, inv) = merge_mat((lower[2], lower[3], lower[4]), (upper[2], upper[3], upper[4]))
    (f, g), w = merge_rhs((lower[0], lower[1]), (upper[0], upper[1]), p, q)
    pay[0], pay[1], pay[2], pay[3], pay[4] = f, g, *stamp
    save[0], save[1], save[2], save[3] = p, q, inv, w


def merge_kernel(axis, bit, mine, other, pay, save):
    side = bit_of(axis, bit)

    @pl.when(side == 0)
    def _():
        merge_all(mine, other, pay, save)

    @pl.when(side == 1)
    def _():
        merge_all(other, mine, pay, save)


def again_all(lower, upper, kept, pay, w_out):
    (f, g), w = merge_rhs((lower[0], lower[1]), (upper[0], upper[1]), kept[0], kept[1])
    pay[0], pay[1] = f, g
    w_out[...] = w


def again_kernel(axis, bit, mine, other, kept, pay, w_out):
    side = bit_of(axis, bit)

    @pl.when(side == 0)
    def _():
        again_all(mine, other, kept, pay, w_out)

    @pl.when(side == 1)
    def _():
        again_all(other, mine, kept, pay, w_out)


def ends_of(axis, levels, sources, f, total):
    x_lo = f / total
    x_hi = jnp.zeros_like(x_lo)
    for bit in reversed(range(len(levels))):
        kept = levels[bit]
        x_mid = kept[0] * x_lo + kept[1] * x_hi + kept[2] * sources[bit]
        upper = jnp.broadcast_to(bit_of(axis, bit), x_lo.shape) == 1
        x_lo, x_hi = jnp.where(upper, x_mid, x_lo), jnp.where(upper, x_hi, x_mid)
    return x_lo, x_hi


def down_local(rows, count, c, x_lo, x_hi, coef, w_of, put):
    def get(j, k):
        return coef[j * (count - 1) + k, :, cut(c)]

    def source(k):
        return w_of[k, :, cut(c)]

    tree_down(0, count, x_lo[:, cut(c)], x_hi[:, cut(c)], get, source, put)


def mid_y_kernel(pay3, s0, s1, s2, cy, w_y, hz_t, hy, hy_u, ex, ie, ch, cz,
                 hz_u, pay, w_out, lo_s, hi_s, f_s, g_s):
    levels = (s0, s1, s2)
    lo_s[...], hi_s[...] = ends_of("gy", levels, [s[3] for s in levels], pay3[0], pay3[2] + pay3[3])
    for c in range(CHUNKS):

        def put(y, x, x_next):
            r = yrow(y, c)
            hz_u[r, :] = hz_t[r, :] + 2.0 * (ch[r, :] * (x_next - x))
            s = hy[plain(y), cut(c)] - hy_u[r, :]
            f_s[r, :] = ie[r, :] * (2.0 * x - ex[plain(y), cut(c)]) + s
            g_s[r, :] = -s

        down_local(yrow, NYL, c, lo_s, hi_s, cy, w_y, put)
        up_local(zrow, NZL, c, f_s, g_s, cz, w_out, pay)


def mid_z_kernel(pay5, s0, s1, s2, s3, s4, cz, w_z, hx_t, hx, ez1, ez, ie, ch, cy,
                 ey1, hx_u, pay, w_out, lo_s, hi_s, f_s, g_s):
    levels = (s0, s1, s2, s3, s4)
    lo_s[...], hi_s[...] = ends_of("gz", levels, [s[3] for s in levels], pay5[0], pay5[2] + pay5[3])
    for c in range(CHUNKS):

        def put(z, x, x_next):
            r = zrow(z, c)
            ey1[r, :] = x
            hx_u[r, :] = hx_t[r, :] + 2.0 * (ch[r, :] * (x_next - x))

        down_local(zrow, NZL, c, lo_s, hi_s, cz, w_z, put)
        for y in range(NYL):
            r = yrow(y, c)
            n = plain(y)
            s = hx[n, cut(c)] - hx_u[r, :]
            f_s[r, :] = ie[r, :] * (2.0 * ez1[n, cut(c)] - ez[n, cut(c)]) + s
            g_s[r, :] = -s
        up_local(yrow, NYL, c, f_s, g_s, cy, w_out, pay)


def end_kernel(axis, rows, count, steps, *refs):
    pay, total = refs[0], refs[1]
    levels, sources = refs[2:2 + steps], refs[2 + steps:2 + 2 * steps]
    coef, w_of, h_u, ch, e_new, h_new, lo_s, hi_s, e_s, h_s = refs[2 + 2 * steps:]
    lo_s[...], hi_s[...] = ends_of(axis, levels, [s[...] for s in sources], pay[0], total[2] + total[3])
    for c in range(CHUNKS):

        def put(i, x, x_next):
            r = rows(i, c)
            e_s[r, :] = x
            h_s[r, :] = h_u[r, :] - ch[r, :] * (x_next - x)

        down_local(rows, count, c, lo_s, hi_s, coef, w_of, put)
        for y in range(NYL):
            e_new[plain(y), cut(c)] = e_s[yrow(y, c), :]
            h_new[plain(y), cut(c)] = h_s[yrow(y, c), :]


def run_row(t):
    return pl.ds(t, 8, stride=RUN)


def x_solve(rhs, ie, ch, cx, keep, x_out, r_t, e_t, h_t, w_s):
    for c in range(CHUNKS):
        r_t[cut(c), :] = rhs[:, cut(c)].T
        if keep:
            e_t[cut(c), :] = tall(ie, c).T
            h_t[cut(c), :] = tall(ch, c).T
    inner = RUN - 1
    merges = inner + 3

    def put_coefs(k, coefs):
        for j in range(3):
            cx[j * merges + k] = coefs[j]

    def get(j, k):
        return cx[j * merges + k]

    def source(k):
        return w_s[k]

    def put_w(k, w):
        w_s[k] = w

    spot = lax.broadcasted_iota(jnp.int32, (8, LANES), 0)
    if keep:
        stamp = tree_mat(0, RUN, lambda t: (e_t[run_row(t), :], h_t[run_row(t), :], None), put_coefs)
        for step in range(3):
            nearby = tuple(pltpu.roll(part, 8 - (1 << step), 0) for part in stamp)
            stamp, coefs = merge_mat(stamp, nearby)
            put_coefs(inner + step, coefs)
        cx[3 * merges] = stamp[0] + stamp[1]
    pair = tree_rhs(0, RUN, lambda t: (r_t[run_row(t), :], jnp.zeros((8, LANES), F32)), get, put_w)
    for step in range(3):
        nearby = tuple(pltpu.roll(part, 8 - (1 << step), 0) for part in pair)
        pair, w = merge_rhs(pair, nearby, get(0, inner + step), get(1, inner + step))
        put_w(inner + step, w)
    x_lo = pair[0] / cx[3 * merges]
    x_hi = jnp.zeros_like(x_lo)
    for step in reversed(range(3)):
        k = inner + step
        x_mid = get(0, k) * x_lo + get(1, k) * x_hi + get(2, k) * source(k)
        upper = ((spot >> step) & 1) == 1
        x_lo, x_hi = (jnp.where(upper, pltpu.roll(x_mid, 1 << step, 0), x_lo),
                      jnp.where(upper, pltpu.roll(x_hi, 1 << step, 0), x_mid))

    def put_x(t, x, x_next):
        r_t[run_row(t), :] = x

    tree_down(0, RUN, x_lo, x_hi, get, source, put_x)
    for c in range(CHUNKS):
        x_out[:, cut(c)] = r_t[cut(c), :].T


def first_x_kernel(hy, ex, ex_rim, hx, hx_rim, ez, ie, ch, ez1, hy_u, cx, r_t, e_t, h_t, w_s, rhs):
    for y in range(NYL):
        r = plain(y)
        ex_r = ex[r, :]
        z_of = lax.broadcasted_iota(jnp.int32, ex_r.shape, 0)
        up = jnp.where(z_of == NZL - 1, jnp.broadcast_to(ex_rim[y:y + 1, :], ex_r.shape), pltpu.roll(ex_r, NZL - 1, 0))
        ht = hy[r, :] - wide(ch, y) * (up - ex_r)
        low = hx[plain(y - 1), :] if y > 0 else hx_rim[...]
        put_wide(hy_u, y, ht)
        rhs[r, :] = wide(ie, y) * ez[r, :] + (ht - prev_x(ht)) - (hx[r, :] - low)
    x_solve(rhs, ie, ch, cx, True, ez1, r_t, e_t, h_t, w_s)
    for y in range(NYL):
        x = ez1[plain(y), :]
        put_wide(hy_u, y, wide(hy_u, y) + 2.0 * (wide(ch, y) * (next_x(x) - x)))


def last_x_kernel(ey1, ey, hz, hz_u, ie, ch, cx, ey_new, hz_new, r_t, w_s, rhs):
    for y in range(NYL):
        r = plain(y)
        s = hz[r, :] - wide(hz_u, y)
        rhs[r, :] = wide(ie, y) * (2.0 * wide(ey1, y) - ey[r, :]) + (s - prev_x(s))
    x_solve(rhs, ie, ch, cx, False, ey_new, r_t, None, None, w_s)
    for y in range(NYL):
        r = plain(y)
        x = ey_new[r, :]
        hz_new[r, :] = wide(hz_u, y) - wide(ch, y) * (next_x(x) - x)


VM = pl.BlockSpec(memory_space=pltpu.VMEM)
SM = pl.BlockSpec(memory_space=pltpu.SMEM)


def shape(*dims):
    return jax.ShapeDtypeStruct(dims, F32)


def call(kernel, args, outs, scratch=(), specs=None, name=None, flops=100000):
    return pl.pallas_call(
        kernel,
        out_shape=[shape(*dims) for dims in outs],
        in_specs=specs or [VM] * len(args),
        out_specs=[VM] * len(outs),
        scratch_shapes=[pltpu.VMEM(dims, F32) for dims in scratch],
        compiler_params=pltpu.CompilerParams(vmem_limit_bytes=40 * 1024 * 1024),
        name=name,
    )(*args)


FIELD = (ROWS, NX)
PACKED = (ROWS * CHUNKS, LANES)
Y1, Z1 = (NZL, NX), (NYL, NX)


def on_device(ex, ey, ez, hx, hy, hz, material, eps_table, mu_table):
    ex, ey, ez, hx, hy, hz, material = (a.reshape(FIELD) for a in (ex, ey, ez, hx, hy, hz, material))

    whole = pl.BlockSpec(FIELD, lambda i: (0, 0))
    hy_top, ez_first, ex_first, hx_last = pl.pallas_call(
        rims_kernel,
        grid=(1,),
        out_shape=[shape(*Z1), shape(*Y1), shape(*Z1), shape(*Y1)],
        in_specs=[whole, pl.BlockSpec(Y1, lambda i: (0, 0)), whole, pl.BlockSpec(Y1, lambda i: (NYL - 1, 0))],
        out_specs=[pl.BlockSpec(Z1, lambda i: (0, 0)), pl.BlockSpec(Y1, lambda i: (0, 0)),
                   pl.BlockSpec(Z1, lambda i: (0, 0)), pl.BlockSpec(Y1, lambda i: (0, 0))],
        name="rims",
    )(hy, ez, ex, hx)
    hy_rim = shifted(hy_top, "gz", 1)
    ez_rim = shifted(ez_first, "gy", -1)
    ex_rim = shifted(ex_first, "gz", -1)
    hx_rim = shifted(hx_last, "gy", 1)

    ie, ch, y_mat, z_mat, cy, cz = call(
        bands_kernel, (material, eps_table, mu_table),
        (PACKED, PACKED, (3,) + Y1, (3,) + Z1, (45,) + Y1, (21,) + Z1), specs=[VM, SM, SM], name="bands")

    pay_y, w_y, hz_t = call(first_y_kernel, (hz, ey, ex, hy, hy_rim, ie, ch, y_mat, cy),
                            ((5,) + Y1, (15,) + Y1, PACKED), (PACKED, PACKED), name="first_y")
    pay_z, w_z, hx_t = call(first_z_kernel, (hx, ez, ez_rim, hz, ey, ie, ch, z_mat, cz),
                            ((5,) + Z1, (7,) + Z1, PACKED), (PACKED, PACKED), name="first_z")

    def merge(pay, axis, step, plane):
        flip, bit = step
        other = swapped(pay, axis, flip)
        return call(functools.partial(merge_kernel, axis, bit), (pay, other), ((5,) + plane, (4,) + plane), name="merge")

    def again(pay, axis, step, plane, kept):
        flip, bit = step
        other = swapped(pay, axis, flip)
        return call(functools.partial(again_kernel, axis, bit), (pay, other, kept), ((2,) + plane, plane), name="again")

    ez1, hy_u, cx = call(first_x_kernel, (hy, ex, ex_rim, hx, hx_rim, ez, ie, ch),
                         (FIELD, PACKED, (3 * (RUN + 2) + 1, 8, LANES)),
                         ((NX, LANES), (NX, LANES), (NX, LANES), (RUN + 2, 8, LANES), FIELD), name="first_x")

    save_y = []
    for step in Y_STEPS:
        pay_y, kept = merge(pay_y, "gy", step, Y1)
        save_y.append(kept)
    hz_u, pay_z2, w_z2 = call(
        mid_y_kernel, (pay_y, *save_y, cy, w_y, hz_t, hy, hy_u, ex, ie, ch, cz),
        (PACKED, (2,) + Z1, (7,) + Z1), (Y1, Y1, PACKED, PACKED), name="mid_y")

    save_z = []
    for step in Z_STEPS:
        pay_z, kept = merge(pay_z, "gz", step, Z1)
        save_z.append(kept)
    ey1, hx_u, pay_y2, w_y2 = call(
        mid_z_kernel, (pay_z, *save_z, cz, w_z, hx_t, hx, ez1, ez, ie, ch, cy),
        (PACKED, PACKED, (2,) + Y1, (15,) + Y1), (Z1, Z1, PACKED, PACKED), name="mid_z")

    from_z = []
    for step, kept in zip(Z_STEPS, save_z):
        pay_z2, w = again(pay_z2, "gz", step, Z1, kept)
        from_z.append(w)
    ex_new, hy_new = call(
        functools.partial(end_kernel, "gz", zrow, NZL, 5), (pay_z2, pay_z, *save_z, *from_z, cz, w_z2, hy_u, ch),
        (FIELD, FIELD), (Z1, Z1, PACKED, PACKED), name="end_z")

    from_y = []
    for step, kept in zip(Y_STEPS, save_y):
        pay_y2, w = again(pay_y2, "gy", step, Y1, kept)
        from_y.append(w)
    ez_new, hx_new = call(
        functools.partial(end_kernel, "gy", yrow, NYL, 3), (pay_y2, pay_y, *save_y, *from_y, cy, w_y2, hx_u, ch),
        (FIELD, FIELD), (Y1, Y1, PACKED, PACKED), name="end_y")

    ey_new, hz_new = call(last_x_kernel, (ey1, ey, hz, hz_u, ie, ch, cx), (FIELD, FIELD),
                          ((NX, LANES), (RUN + 2, 8, LANES), FIELD), name="last_x")

    return tuple(a.reshape(NYL, NZL, NX) for a in (ex_new, ey_new, ez_new, hx_new, hy_new, hz_new))


def solution(mesh):
    cells = P("gy", "gz", None)
    return jax.shard_map(
        on_device,
        mesh=mesh,
        in_specs=(cells,) * 7 + (P(), P()),
        out_specs=(cells,) * 6,
        check_vma=False,
    )
```

```python
import functools

import jax
import jax.numpy as jnp
from jax import lax
from jax.experimental import pallas as pl
from jax.experimental.pallas import tpu as pltpu
from jax.sharding import PartitionSpec as P

courant = 16.0
F32 = jnp.float32
NYL, NZL, NX = 16, 8, 512
ROWS = NYL * NZL
LANES = 128
CHUNKS = NX // LANES
RUN = NX // 8

Y_STEPS = ((1, 0), (2, 1), (6, 2))
Z_STEPS = ((1, 0), (2, 1), (6, 2), (8, 3), (24, 4))


def met(array, axis, first):
    size = lax.axis_size(axis)
    low = range(first, size - 1, 2)
    return lax.ppermute(array, axis, [(i, i + 1) for i in low] + [(i + 1, i) for i in low])


def swapped(array, axis, flip):
    size = lax.axis_size(axis)
    return lax.ppermute(array, axis, [(i, i ^ flip) for i in range(size)])


def merge_mat(s1, s2):
    ga1, b1, gc1 = s1
    ga2, b2, gc2 = s2
    ground = ga2 if gc1 is None else gc1 + ga2
    inv = 1.0 / (b1 + b2 + ground)
    p, q = b1 * inv, b2 * inv
    right = q * ground
    return (ga1 + p * ground, p * b2, right if gc2 is None else gc2 + right), (p, q, inv)


def merge_rhs(r1, r2, p, q):
    w = r1[1] + r2[0]
    return (r1[0] + p * w, r2[1] + q * w), w


def tree_mat(lo, hi, leaf, put):
    if hi - lo == 1:
        return leaf(lo)
    mid = (lo + hi) // 2
    left = tree_mat(lo, mid, leaf, put)
    right = tree_mat(mid, hi, leaf, put)
    stamp, coefs = merge_mat(left, right)
    put(mid - 1, coefs)
    return stamp


def tree_rhs(lo, hi, leaf, coef, put):
    if hi - lo == 1:
        return leaf(lo)
    mid = (lo + hi) // 2
    left = tree_rhs(lo, mid, leaf, coef, put)
    right = tree_rhs(mid, hi, leaf, coef, put)
    out, w = merge_rhs(left, right, coef(0, mid - 1), coef(1, mid - 1))
    put(mid - 1, w)
    return out


def tree_down(lo, hi, x_lo, x_hi, coef, source, put):
    if hi - lo == 1:
        put(lo, x_lo, x_hi)
        return
    mid = (lo + hi) // 2
    k = mid - 1
    x_mid = coef(0, k) * x_lo + coef(1, k) * x_hi + coef(2, k) * source(k)
    tree_down(lo, mid, x_lo, x_mid, coef, source, put)
    tree_down(mid, hi, x_mid, x_hi, coef, source, put)


def cut(c):
    return pl.ds(c * LANES, LANES)


def plain(y):
    return pl.ds(y * NZL, NZL)


def yrow(y, c):
    return pl.ds((y * CHUNKS + c) * NZL, NZL)


def zrow(z, c):
    return pl.ds(c * NZL + z, NYL, stride=CHUNKS * NZL)


def wide(ref, y):
    return jnp.concatenate([ref[yrow(y, c), :] for c in range(CHUNKS)], axis=1)


def put_wide(ref, y, value):
    for c in range(CHUNKS):
        ref[yrow(y, c), :] = value[:, c * LANES:(c + 1) * LANES]


def tall(ref, c):
    return jnp.concatenate([ref[yrow(y, c), :] for y in range(NYL)], axis=0)


def next_x(v):
    lane = lax.broadcasted_iota(jnp.int32, v.shape, 1)
    return jnp.where(lane == NX - 1, 0.0, pltpu.roll(v, NX - 1, 1))


def prev_x(v):
    lane = lax.broadcasted_iota(jnp.int32, v.shape, 1)
    return jnp.where(lane == 0, 0.0, pltpu.roll(v, 1, 1))


def bit_of(axis, bit):
    return (lax.axis_index(axis) >> bit) & 1


def inputs_kernel(*refs):
    away, (eps, mu), here = refs[:7], refs[7:9], refs[9:16]
    y_even, y_odd, z_even, z_odd, tables, eps_s, mu_s, sems = refs[16:]
    copies = [pltpu.make_async_copy(away[i], here[i], sems.at[i]) for i in range(7)]
    copies.append(pltpu.make_async_copy(eps, eps_s, sems.at[7]))
    copies.append(pltpu.make_async_copy(mu, mu_s, sems.at[8]))
    for copy in copies:
        copy.start()
    for copy in copies:
        copy.wait()
    ex, ez, hx, hy = here[0], here[2], here[3], here[4]

    def fill(axis, low, high, even, odd):
        up = (lax.axis_index(axis) & 1) == 0

        @pl.when(up)
        def _():
            low(even)
            high(odd)

        @pl.when(jnp.logical_not(up))
        def _():
            high(even)
            low(odd)

    def hx_last(out):
        out[...] = hx[plain(NYL - 1), :]

    def ez_first(out):
        out[...] = ez[plain(0), :]

    def hy_last(out):
        for y in range(NYL):
            out[y:y + 1, :] = hy[(y + 1) * NZL - 1:(y + 1) * NZL, :]

    def ex_first(out):
        for y in range(NYL):
            out[y:y + 1, :] = ex[y * NZL:y * NZL + 1, :]

    fill("gy", hx_last, ez_first, y_even, y_odd)
    fill("gz", hy_last, ex_first, z_even, z_odd)
    for k in range(16):
        tables[k:k + 1, :] = jnp.full((1, LANES), eps_s[k], F32)
        tables[16 + k:17 + k, :] = jnp.full((1, LANES), mu_s[k], F32)


def from_below(axis, even, odd):
    return jnp.where(jnp.broadcast_to(lax.axis_index(axis) & 1, even.shape) == 1, even, odd)


def from_above(axis, even, odd):
    return jnp.where(jnp.broadcast_to(lax.axis_index(axis) & 1, even.shape) == 0, even, odd)


def bands_kernel(material, tables, ie, ch, y_mat, z_mat, cy, cz):
    spread = [jnp.broadcast_to(tables[k:k + 1, :], (NZL, LANES)) for k in range(32)]
    for y in range(NYL):
        for c in range(CHUNKS):
            label = material[plain(y), cut(c)]
            e_val, m_val = spread[0], spread[16]
            for k in range(1, 16):
                hit = label == k
                e_val = jnp.where(hit, spread[k], e_val)
                m_val = jnp.where(hit, spread[16 + k], m_val)
            ie[yrow(y, c), :] = e_val * (1.0 / courant)
            ch[yrow(y, c), :] = courant / m_val
    for c in range(CHUNKS):
        for rows, count, mat, coef in ((yrow, NYL, y_mat, cy), (zrow, NZL, z_mat, cz)):

            def leaf(i):
                return ie[rows(i, c), :], ch[rows(i, c), :], None

            def put(k, coefs):
                for j in range(3):
                    coef[j * (count - 1) + k, :, cut(c)] = coefs[j]

            for j, part in enumerate(tree_mat(0, count, leaf, put)):
                mat[j, :, cut(c)] = part


def up_local(rows, count, c, f_of, g_of, coef, w_out, pay):
    def leaf(i):
        return f_of[rows(i, c), :], g_of[rows(i, c), :]

    def get(j, k):
        return coef[j * (count - 1) + k, :, cut(c)]

    def put(k, w):
        w_out[k, :, cut(c)] = w

    f, g = tree_rhs(0, count, leaf, get, put)
    pay[0, :, cut(c)] = f
    pay[1, :, cut(c)] = g


def first_y_kernel(hz, ey, ex, hy, z_even, z_odd, ie, ch, y_mat, cy, pay, w_out, hz_t, f_s, g_s, hy_rim):
    hy_rim[...] = from_below("gz", z_even[...], z_odd[...])
    for y in range(NYL):
        r = plain(y)
        ey_r = ey[r, :]
        ht = hz[r, :] - wide(ch, y) * (next_x(ey_r) - ey_r)
        hy_r = hy[r, :]
        z_of = lax.broadcasted_iota(jnp.int32, hy_r.shape, 0)
        low = jnp.where(z_of == 0, jnp.broadcast_to(hy_rim[y:y + 1, :], hy_r.shape), pltpu.roll(hy_r, 1, 0))
        put_wide(hz_t, y, ht)
        put_wide(f_s, y, wide(ie, y) * ex[r, :] - (hy_r - low) + ht)
        put_wide(g_s, y, -ht)
    for c in range(CHUNKS):
        up_local(yrow, NYL, c, f_s, g_s, cy, w_out, pay)
    pay[2:5] = y_mat[...]


def first_z_kernel(hx, ez, y_even, y_odd, hz, ey, ie, ch, z_mat, cz, pay, w_out, hx_t, f_s, g_s):
    for y in range(NYL):
        r = plain(y)
        up = ez[plain(y + 1), :] if y < NYL - 1 else from_above("gy", y_even[...], y_odd[...])
        ht = hx[r, :] - wide(ch, y) * (up - ez[r, :])
        hz_r = hz[r, :]
        put_wide(hx_t, y, ht)
        put_wide(f_s, y, wide(ie, y) * ey[r, :] - (hz_r - prev_x(hz_r)) + ht)
        put_wide(g_s, y, -ht)
    for c in range(CHUNKS):
        up_local(zrow, NZL, c, f_s, g_s, cz, w_out, pay)
    pay[2:5] = z_mat[...]


def merge_all(axis, top, lower, upper, pay, save, edge):
    stamp, (p, q, inv) = merge_mat((lower[2], lower[3], lower[4]), (upper[2], upper[3], upper[4]))
    (f, g), w = merge_rhs((lower[0], lower[1]), (upper[0], upper[1]), p, q)
    save[0], save[1], save[2], save[3] = p, q, inv, w
    if top is None:
        pay[0], pay[1], pay[2], pay[3], pay[4] = f, g, *stamp
        return
    ga, b, gc = stamp
    share = 1.0 / (ga + b)
    reach = b * share
    high = jnp.broadcast_to(bit_of(axis, top), f.shape) == 1
    pay[0] = jnp.where(high, f, g + reach * f)
    pay[1] = jnp.where(high, ga + b, gc + reach * ga)
    edge[0], edge[1], edge[2] = reach, share, f


def merge_kernel(axis, bit, top, mine, other, pay, save, edge=None):
    side = bit_of(axis, bit)

    @pl.when(side == 0)
    def _():
        merge_all(axis, top, mine, other, pay, save, edge)

    @pl.when(side == 1)
    def _():
        merge_all(axis, top, other, mine, pay, save, edge)


def again_all(axis, top, lower, upper, kept, edge, pay, w_out, f_out):
    (f, g), w = merge_rhs((lower[0], lower[1]), (upper[0], upper[1]), kept[0], kept[1])
    w_out[...] = w
    if top is None:
        pay[0], pay[1] = f, g
        return
    high = jnp.broadcast_to(bit_of(axis, top), f.shape) == 1
    pay[...] = jnp.where(high, f, g + edge[0] * f)
    f_out[...] = f


def again_kernel(axis, bit, mine, other, kept, pay, w_out):
    side = bit_of(axis, bit)

    @pl.when(side == 0)
    def _():
        again_all(axis, None, mine, other, kept, None, pay, w_out, None)

    @pl.when(side == 1)
    def _():
        again_all(axis, None, other, mine, kept, None, pay, w_out, None)


def again_top_kernel(axis, bit, top, mine, other, kept, edge, pay, w_out, f_out):
    side = bit_of(axis, bit)

    @pl.when(side == 0)
    def _():
        again_all(axis, top, mine, other, kept, edge, pay, w_out, f_out)

    @pl.when(side == 1)
    def _():
        again_all(axis, top, other, mine, kept, edge, pay, w_out, f_out)


def ends_of(axis, x_meet, reach, share, f, levels, sources):
    high = jnp.broadcast_to(bit_of(axis, len(levels)), x_meet.shape) == 1
    x_lo = jnp.where(high, x_meet, share * f + reach * x_meet)
    x_hi = jnp.where(high, 0.0, x_meet)
    for bit in reversed(range(len(levels))):
        kept = levels[bit]
        x_mid = kept[0] * x_lo + kept[1] * x_hi + kept[2] * sources[bit]
        upper = jnp.broadcast_to(bit_of(axis, bit), x_lo.shape) == 1
        x_lo, x_hi = jnp.where(upper, x_mid, x_lo), jnp.where(upper, x_hi, x_mid)
    return x_lo, x_hi


def first_ends(axis, mine, other, edge, levels, inv):
    inv[...] = 1.0 / (mine[1] + other[1])
    return ends_of(axis, (mine[0] + other[0]) * inv[...], edge[0], edge[1], edge[2], levels, [s[3] for s in levels])


def down_local(rows, count, c, x_lo, x_hi, coef, w_of, put):
    def get(j, k):
        return coef[j * (count - 1) + k, :, cut(c)]

    def source(k):
        return w_of[k, :, cut(c)]

    tree_down(0, count, x_lo[:, cut(c)], x_hi[:, cut(c)], get, source, put)


def mid_y_kernel(mine, other, edge, s0, s1, cy, w_y, hz_t, hy, hy_u, ex, ie, ch, cz,
                 hz_u, pay, w_out, inv, lo_s, hi_s, f_s, g_s):
    lo_s[...], hi_s[...] = first_ends("gy", mine, other, edge, (s0, s1), inv)
    for c in range(CHUNKS):

        def put(y, x, x_next):
            r = yrow(y, c)
            hz_u[r, :] = hz_t[r, :] + 2.0 * (ch[r, :] * (x_next - x))
            s = hy[plain(y), cut(c)] - hy_u[r, :]
            f_s[r, :] = ie[r, :] * (2.0 * x - ex[plain(y), cut(c)]) + s
            g_s[r, :] = -s

        down_local(yrow, NYL, c, lo_s, hi_s, cy, w_y, put)
        up_local(zrow, NZL, c, f_s, g_s, cz, w_out, pay)


def mid_z_kernel(mine, other, edge, s0, s1, s2, s3, cz, w_z, hx_t, hx, ez1, ez, ie, ch, cy,
                 ey1, hx_u, pay, w_out, inv, lo_s, hi_s, f_s, g_s):
    lo_s[...], hi_s[...] = first_ends("gz", mine, other, edge, (s0, s1, s2, s3), inv)
    for c in range(CHUNKS):

        def put(z, x, x_next):
            r = zrow(z, c)
            ey1[r, :] = x
            hx_u[r, :] = hx_t[r, :] + 2.0 * (ch[r, :] * (x_next - x))

        down_local(zrow, NZL, c, lo_s, hi_s, cz, w_z, put)
        for y in range(NYL):
            r = yrow(y, c)
            n = plain(y)
            s = hx[n, cut(c)] - hx_u[r, :]
            f_s[r, :] = ie[r, :] * (2.0 * ez1[n, cut(c)] - ez[n, cut(c)]) + s
            g_s[r, :] = -s
        up_local(yrow, NYL, c, f_s, g_s, cy, w_out, pay)


def end_kernel(axis, rows, count, steps, *refs):
    mine, other, inv, edge, f = refs[:5]
    levels, sources = refs[5:5 + steps], refs[5 + steps:5 + 2 * steps]
    coef, w_of, h_u, ch, e_new, h_new, done, lo_s, hi_s, e_s, h_s = refs[5 + 2 * steps:]
    done[...] = jnp.zeros_like(done)
    lo_s[...], hi_s[...] = ends_of(axis, (mine[...] + other[...]) * inv[...], edge[0], edge[1], f[...], levels,
                                   [s[...] for s in sources])
    for c in range(CHUNKS):

        def put(i, x, x_next):
            r = rows(i, c)
            e_s[r, :] = x
            h_s[r, :] = h_u[r, :] - ch[r, :] * (x_next - x)

        down_local(rows, count, c, lo_s, hi_s, coef, w_of, put)
        for y in range(NYL):
            e_new[plain(y), cut(c)] = e_s[yrow(y, c), :]
            h_new[plain(y), cut(c)] = h_s[yrow(y, c), :]


def run_row(t):
    return pl.ds(t, 8, stride=RUN)


def x_solve(rhs, ie, ch, cx, keep, x_out, r_t, e_t, h_t, w_s):
    for c in range(CHUNKS):
        r_t[cut(c), :] = rhs[:, cut(c)].T
        if keep:
            e_t[cut(c), :] = tall(ie, c).T
            h_t[cut(c), :] = tall(ch, c).T
    inner = RUN - 1
    merges = inner + 3

    def put_coefs(k, coefs):
        for j in range(3):
            cx[j * merges + k] = coefs[j]

    def get(j, k):
        return cx[j * merges + k]

    def source(k):
        return w_s[k]

    def put_w(k, w):
        w_s[k] = w

    spot = lax.broadcasted_iota(jnp.int32, (8, LANES), 0)
    if keep:
        stamp = tree_mat(0, RUN, lambda t: (e_t[run_row(t), :], h_t[run_row(t), :], None), put_coefs)
        for step in range(3):
            nearby = tuple(pltpu.roll(part, 8 - (1 << step), 0) for part in stamp)
            stamp, coefs = merge_mat(stamp, nearby)
            put_coefs(inner + step, coefs)
        cx[3 * merges] = stamp[0] + stamp[1]
    pair = tree_rhs(0, RUN, lambda t: (r_t[run_row(t), :], jnp.zeros((8, LANES), F32)), get, put_w)
    for step in range(3):
        nearby = tuple(pltpu.roll(part, 8 - (1 << step), 0) for part in pair)
        pair, w = merge_rhs(pair, nearby, get(0, inner + step), get(1, inner + step))
        put_w(inner + step, w)
    x_lo = pair[0] / cx[3 * merges]
    x_hi = jnp.zeros_like(x_lo)
    for step in reversed(range(3)):
        k = inner + step
        x_mid = get(0, k) * x_lo + get(1, k) * x_hi + get(2, k) * source(k)
        upper = ((spot >> step) & 1) == 1
        x_lo, x_hi = (jnp.where(upper, pltpu.roll(x_mid, 1 << step, 0), x_lo),
                      jnp.where(upper, pltpu.roll(x_hi, 1 << step, 0), x_mid))

    def put_x(t, x, x_next):
        r_t[run_row(t), :] = x

    tree_down(0, RUN, x_lo, x_hi, get, source, put_x)
    for c in range(CHUNKS):
        x_out[:, cut(c)] = r_t[cut(c), :].T


def first_x_kernel(hy, ex, z_even, z_odd, hx, y_even, y_odd, ez, ie, ch, ez1, hy_u, cx, r_t, e_t, h_t, w_s, rhs, ex_rim):
    ex_rim[...] = from_above("gz", z_even[...], z_odd[...])
    for y in range(NYL):
        r = plain(y)
        ex_r = ex[r, :]
        z_of = lax.broadcasted_iota(jnp.int32, ex_r.shape, 0)
        up = jnp.where(z_of == NZL - 1, jnp.broadcast_to(ex_rim[y:y + 1, :], ex_r.shape), pltpu.roll(ex_r, NZL - 1, 0))
        ht = hy[r, :] - wide(ch, y) * (up - ex_r)
        low = hx[plain(y - 1), :] if y > 0 else from_below("gy", y_even[...], y_odd[...])
        put_wide(hy_u, y, ht)
        rhs[r, :] = wide(ie, y) * ez[r, :] + (ht - prev_x(ht)) - (hx[r, :] - low)
    x_solve(rhs, ie, ch, cx, True, ez1, r_t, e_t, h_t, w_s)
    for y in range(NYL):
        x = ez1[plain(y), :]
        put_wide(hy_u, y, wide(hy_u, y) + 2.0 * (wide(ch, y) * (next_x(x) - x)))


def last_x_kernel(ey1, ey, hz, hz_u, ie, ch, cx, ey_new, hz_new, done, r_t, w_s, rhs):
    done[...] = jnp.zeros_like(done)
    for y in range(NYL):
        r = plain(y)
        s = hz[r, :] - wide(hz_u, y)
        rhs[r, :] = wide(ie, y) * (2.0 * wide(ey1, y) - ey[r, :]) + (s - prev_x(s))
    x_solve(rhs, ie, ch, cx, False, ey_new, r_t, None, None, w_s)
    for y in range(NYL):
        r = plain(y)
        x = ey_new[r, :]
        hz_new[r, :] = wide(hz_u, y) - wide(ch, y) * (next_x(x) - x)


VM = pl.BlockSpec(memory_space=pltpu.VMEM)


def shape(*dims):
    return jax.ShapeDtypeStruct(dims, F32)


class Order:
    def __init__(self):
        self.last = None

    def __call__(self, kernel, args, outs, scratch=(), specs=None, after=(), name=None):
        after = list(after) + ([] if self.last is None else [self.last])
        count = len(args)

        def body(*refs):
            kernel(*refs[:count], *refs[count + len(after):])

        results = pl.pallas_call(
            body,
            out_shape=[shape(*dims) for dims in outs],
            in_specs=(specs or [VM] * count) + [pl.BlockSpec(memory_space=pl.ANY)] * len(after),
            out_specs=[VM] * len(outs),
            scratch_shapes=[pltpu.VMEM(dims, F32) for dims in scratch],
            compiler_params=pltpu.CompilerParams(vmem_limit_bytes=16 * 1024 * 1024),
            name=name,
        )(*args, *after)
        self.last = results[-1]
        return results


FIELD = (ROWS, NX)
PACKED = (ROWS * CHUNKS, LANES)
Y1, Z1 = (NZL, NX), (NYL, NX)


def on_device(ex, ey, ez, hx, hy, hz, material, eps_table, mu_table):
    ex, ey, ez, hx, hy, hz, material = (a.reshape(FIELD) for a in (ex, ey, ez, hx, hy, hz, material))

    call = Order()

    inputs = (ex, ey, ez, hx, hy, hz, material)
    ex, ey, ez, hx, hy, hz, material, y_even, y_odd, z_even, z_odd, tables = pl.pallas_call(
        inputs_kernel,
        out_shape=[jax.ShapeDtypeStruct(FIELD, a.dtype) for a in inputs]
        + [shape(*Y1), shape(*Y1), shape(*Z1), shape(*Z1), shape(32, LANES)],
        in_specs=[pl.BlockSpec(memory_space=pltpu.HBM)] * 9,
        out_specs=[VM] * 12,
        scratch_shapes=[pltpu.SMEM((16,), F32), pltpu.SMEM((16,), F32), pltpu.SemaphoreType.DMA((9,))],
        compiler_params=pltpu.CompilerParams(vmem_limit_bytes=52 * 1024 * 1024),
        name="inputs",
    )(*inputs, eps_table, mu_table)
    y_even, z_even = met(y_even, "gy", 0), met(z_even, "gz", 0)
    y_odd, z_odd = met(y_odd, "gy", 1), met(z_odd, "gz", 1)

    ie, ch, y_mat, z_mat, cy, cz = call(
        bands_kernel, (material, tables),
        (PACKED, PACKED, (3,) + Y1, (3,) + Z1, (45,) + Y1, (21,) + Z1), name="bands")

    pay_z, w_z, hx_t = call(first_z_kernel, (hx, ez, y_even, y_odd, hz, ey, ie, ch, z_mat, cz),
                            ((5,) + Z1, (7,) + Z1, PACKED), (PACKED, PACKED), after=(z_even, z_odd), name="first_z")
    pay_y, w_y, hz_t = call(first_y_kernel, (hz, ey, ex, hy, z_even, z_odd, ie, ch, y_mat, cy),
                            ((5,) + Y1, (15,) + Y1, PACKED), (PACKED, PACKED, Z1), name="first_y")

    def merge(pay, axis, step, plane, saved, top=None):
        flip, bit = step
        other = swapped(pay, axis, flip)
        kernel = functools.partial(merge_kernel, axis, bit, top)
        if top is None:
            pay, kept = call(kernel, (pay, other), ((5,) + plane, (4,) + plane), name="merge_" + axis)
            saved.append(kept)
            return pay
        pay, kept, edge = call(kernel, (pay, other), ((2,) + plane, (4,) + plane, (3,) + plane), name="merge_" + axis)
        saved.append(kept)
        return pay, edge

    def again(pay, axis, step, plane, kept, sources, top=None, edge=None):
        flip, bit = step
        other = swapped(pay, axis, flip)
        if top is None:
            pay, w = call(functools.partial(again_kernel, axis, bit), (pay, other, kept), ((2,) + plane, plane),
                          name="again_" + axis)
            sources.append(w)
            return pay
        pay, w, f = call(functools.partial(again_top_kernel, axis, bit, top), (pay, other, kept, edge),
                         (plane, plane, plane), name="again_" + axis)
        sources.append(w)
        return pay, f

    save_z, save_y, from_z, from_y = [], [], [], []
    pay_z = merge(pay_z, "gz", Z_STEPS[0], Z1, save_z)
    pay_y = merge(pay_y, "gy", Y_STEPS[0], Y1, save_y)
    ez1, hy_u, cx = call(first_x_kernel, (hy, ex, z_even, z_odd, hx, y_even, y_odd, ez, ie, ch),
                         (FIELD, PACKED, (3 * (RUN + 2) + 1, 8, LANES)),
                         ((NX, LANES), (NX, LANES), (NX, LANES), (RUN + 2, 8, LANES), FIELD, Z1), name="first_x")
    pay_z = merge(pay_z, "gz", Z_STEPS[1], Z1, save_z)
    pay_y, edge_y = merge(pay_y, "gy", Y_STEPS[1], Y1, save_y, Y_STEPS[2][1])
    pay_z = merge(pay_z, "gz", Z_STEPS[2], Z1, save_z)
    hz_u, pay_z2, w_z2, inv_y = call(
        mid_y_kernel, (pay_y, swapped(pay_y, "gy", Y_STEPS[2][0]), edge_y, *save_y, cy, w_y, hz_t, hy, hy_u, ex, ie, ch, cz),
        (PACKED, (2,) + Z1, (7,) + Z1, Y1), (Y1, Y1, PACKED, PACKED), name="mid_y")
    pay_z, edge_z = merge(pay_z, "gz", Z_STEPS[3], Z1, save_z, Z_STEPS[4][1])
    pay_z2 = again(pay_z2, "gz", Z_STEPS[0], Z1, save_z[0], from_z)
    ey1, hx_u, pay_y2, w_y2, inv_z = call(
        mid_z_kernel, (pay_z, swapped(pay_z, "gz", Z_STEPS[4][0]), edge_z, *save_z, cz, w_z, hx_t, hx, ez1, ez, ie, ch, cy),
        (PACKED, PACKED, (2,) + Y1, (15,) + Y1, Z1), (Z1, Z1, PACKED, PACKED), name="mid_z")
    pay_z2 = again(pay_z2, "gz", Z_STEPS[1], Z1, save_z[1], from_z)
    pay_y2 = again(pay_y2, "gy", Y_STEPS[0], Y1, save_y[0], from_y)
    pay_z2 = again(pay_z2, "gz", Z_STEPS[2], Z1, save_z[2], from_z)
    pay_y2, f_y = again(pay_y2, "gy", Y_STEPS[1], Y1, save_y[1], from_y, Y_STEPS[2][1], edge_y)
    pay_z2, f_z = again(pay_z2, "gz", Z_STEPS[3], Z1, save_z[3], from_z, Z_STEPS[4][1], edge_z)
    mark = (8, LANES)
    ey_new, hz_new, _ = call(last_x_kernel, (ey1, ey, hz, hz_u, ie, ch, cx), (FIELD, FIELD, mark),
                             ((NX, LANES), (RUN + 2, 8, LANES), FIELD), name="last_x")
    ez_new, hx_new, _ = call(
        functools.partial(end_kernel, "gy", yrow, NYL, 2),
        (pay_y2, swapped(pay_y2, "gy", Y_STEPS[2][0]), inv_y, edge_y, f_y, *save_y, *from_y, cy, w_y2, hx_u, ch),
        (FIELD, FIELD, mark), (Y1, Y1, PACKED, PACKED), name="end_y")
    ex_new, hy_new, _ = call(
        functools.partial(end_kernel, "gz", zrow, NZL, 4),
        (pay_z2, swapped(pay_z2, "gz", Z_STEPS[4][0]), inv_z, edge_z, f_z, *save_z, *from_z, cz, w_z2, hy_u, ch),
        (FIELD, FIELD, mark), (Z1, Z1, PACKED, PACKED), name="end_z")

    return tuple(a.reshape(NYL, NZL, NX) for a in (ex_new, ey_new, ez_new, hx_new, hy_new, hz_new))


def solution(mesh):
    cells = P("gy", "gz", None)
    return jax.shard_map(
        on_device,
        mesh=mesh,
        in_specs=(cells,) * 7 + (P(), P()),
        out_specs=(cells,) * 6,
        check_vma=False,
    )
```

```python
import functools

import jax
import jax.numpy as jnp
from jax import lax
from jax.experimental import pallas as pl
from jax.experimental.pallas import tpu as pltpu
from jax.sharding import PartitionSpec as P

courant = 16.0
F32 = jnp.float32
NYL, NZL, NX = 16, 8, 512
ROWS = NYL * NZL
LANES = 128
CHUNKS = NX // LANES
RUN = NX // 8

Y_STEPS = ((1, 0), (2, 1), (6, 2))
Z_STEPS = ((1, 0), (2, 1), (6, 2), (8, 3), (24, 4))


def met(array, axis, first):
    size = lax.axis_size(axis)
    low = range(first, size - 1, 2)
    return lax.ppermute(array, axis, [(i, i + 1) for i in low] + [(i + 1, i) for i in low])


def swapped(array, axis, flip):
    size = lax.axis_size(axis)
    return lax.ppermute(array, axis, [(i, i ^ flip) for i in range(size)])


def merge_mat(s1, s2):
    ga1, b1, gc1 = s1
    ga2, b2, gc2 = s2
    ground = ga2 if gc1 is None else gc1 + ga2
    inv = 1.0 / (b1 + b2 + ground)
    p, q = b1 * inv, b2 * inv
    right = q * ground
    return (ga1 + p * ground, p * b2, right if gc2 is None else gc2 + right), (p, q, inv)


def merge_rhs(r1, r2, p, q):
    w = r1[1] + r2[0]
    return (r1[0] + p * w, r2[1] + q * w), w


def tree_mat(lo, hi, leaf, put):
    if hi - lo == 1:
        return leaf(lo)
    mid = (lo + hi) // 2
    left = tree_mat(lo, mid, leaf, put)
    right = tree_mat(mid, hi, leaf, put)
    stamp, coefs = merge_mat(left, right)
    put(mid - 1, coefs)
    return stamp


def tree_rhs(lo, hi, leaf, coef, put):
    if hi - lo == 1:
        return leaf(lo)
    mid = (lo + hi) // 2
    left = tree_rhs(lo, mid, leaf, coef, put)
    right = tree_rhs(mid, hi, leaf, coef, put)
    out, w = merge_rhs(left, right, coef(0, mid - 1), coef(1, mid - 1))
    put(mid - 1, w)
    return out


def tree_down(lo, hi, x_lo, x_hi, coef, source, put):
    if hi - lo == 1:
        put(lo, x_lo, x_hi)
        return
    mid = (lo + hi) // 2
    k = mid - 1
    x_mid = coef(0, k) * x_lo + coef(1, k) * x_hi + coef(2, k) * source(k)
    tree_down(lo, mid, x_lo, x_mid, coef, source, put)
    tree_down(mid, hi, x_mid, x_hi, coef, source, put)


def cut(c):
    return pl.ds(c * LANES, LANES)


def plain(y):
    return pl.ds(y * NZL, NZL)


def yrow(y, c):
    return pl.ds((y * CHUNKS + c) * NZL, NZL)


def zrow(z, c):
    return pl.ds(c * NZL + z, NYL, stride=CHUNKS * NZL)


def wide(ref, y):
    return jnp.concatenate([ref[yrow(y, c), :] for c in range(CHUNKS)], axis=1)


def put_wide(ref, y, value):
    for c in range(CHUNKS):
        ref[yrow(y, c), :] = value[:, c * LANES:(c + 1) * LANES]


def tall(ref, c):
    return jnp.concatenate([ref[yrow(y, c), :] for y in range(NYL)], axis=0)


def next_x(v):
    lane = lax.broadcasted_iota(jnp.int32, v.shape, 1)
    return jnp.where(lane == NX - 1, 0.0, pltpu.roll(v, NX - 1, 1))


def prev_x(v):
    lane = lax.broadcasted_iota(jnp.int32, v.shape, 1)
    return jnp.where(lane == 0, 0.0, pltpu.roll(v, 1, 1))


def bit_of(axis, bit):
    return (lax.axis_index(axis) >> bit) & 1


def inputs_kernel(*refs):
    away, (eps, mu), here = refs[:7], refs[7:9], refs[9:16]
    y_even, y_odd, z_even, z_odd, tables, eps_s, mu_s, sems = refs[16:]
    copies = [pltpu.make_async_copy(away[i], here[i], sems.at[i]) for i in range(7)]
    copies.append(pltpu.make_async_copy(eps, eps_s, sems.at[7]))
    copies.append(pltpu.make_async_copy(mu, mu_s, sems.at[8]))
    for copy in copies:
        copy.start()
    for copy in copies:
        copy.wait()
    ex, ez, hx, hy = here[0], here[2], here[3], here[4]

    def fill(axis, low, high, even, odd):
        up = (lax.axis_index(axis) & 1) == 0

        @pl.when(up)
        def _():
            low(even)
            high(odd)

        @pl.when(jnp.logical_not(up))
        def _():
            high(even)
            low(odd)

    def hx_last(out):
        out[...] = hx[plain(NYL - 1), :]

    def ez_first(out):
        out[...] = ez[plain(0), :]

    def hy_last(out):
        for y in range(NYL):
            out[y:y + 1, :] = hy[(y + 1) * NZL - 1:(y + 1) * NZL, :]

    def ex_first(out):
        for y in range(NYL):
            out[y:y + 1, :] = ex[y * NZL:y * NZL + 1, :]

    fill("gy", hx_last, ez_first, y_even, y_odd)
    fill("gz", hy_last, ex_first, z_even, z_odd)
    for k in range(16):
        tables[k:k + 1, :] = jnp.full((1, LANES), eps_s[k], F32)
        tables[16 + k:17 + k, :] = jnp.full((1, LANES), mu_s[k], F32)


def from_below(axis, even, odd):
    return jnp.where(jnp.broadcast_to(lax.axis_index(axis) & 1, even.shape) == 1, even, odd)


def from_above(axis, even, odd):
    return jnp.where(jnp.broadcast_to(lax.axis_index(axis) & 1, even.shape) == 0, even, odd)


def bands_kernel(material, tables, ie, ch, y_mat, z_mat, cy, cz):
    spread = [jnp.broadcast_to(tables[k:k + 1, :], (NZL, LANES)) for k in range(32)]
    for y in range(NYL):
        for c in range(CHUNKS):
            label = material[plain(y), cut(c)]
            e_val, m_val = spread[0], spread[16]
            for k in range(1, 16):
                hit = label == k
                e_val = jnp.where(hit, spread[k], e_val)
                m_val = jnp.where(hit, spread[16 + k], m_val)
            ie[yrow(y, c), :] = e_val * (1.0 / courant)
            ch[yrow(y, c), :] = courant / m_val
    for c in range(CHUNKS):
        for rows, count, mat, coef in ((yrow, NYL, y_mat, cy), (zrow, NZL, z_mat, cz)):

            def leaf(i):
                return ie[rows(i, c), :], ch[rows(i, c), :], None

            def put(k, coefs):
                for j in range(3):
                    coef[j * (count - 1) + k, :, cut(c)] = coefs[j]

            for j, part in enumerate(tree_mat(0, count, leaf, put)):
                mat[j, :, cut(c)] = part


def up_local(rows, count, c, f_of, g_of, coef, w_out, pay):
    def leaf(i):
        return f_of[rows(i, c), :], g_of[rows(i, c), :]

    def get(j, k):
        return coef[j * (count - 1) + k, :, cut(c)]

    def put(k, w):
        w_out[k, :, cut(c)] = w

    f, g = tree_rhs(0, count, leaf, get, put)
    pay[0, :, cut(c)] = f
    pay[1, :, cut(c)] = g


def first_y_kernel(hz, ey, ex, hy, z_even, z_odd, ie, ch, y_mat, cy, pay, w_out, hz_t, f_s, g_s, hy_rim):
    hy_rim[...] = from_below("gz", z_even[...], z_odd[...])
    for y in range(NYL):
        r = plain(y)
        ey_r = ey[r, :]
        ht = hz[r, :] - wide(ch, y) * (next_x(ey_r) - ey_r)
        hy_r = hy[r, :]
        z_of = lax.broadcasted_iota(jnp.int32, hy_r.shape, 0)
        low = jnp.where(z_of == 0, jnp.broadcast_to(hy_rim[y:y + 1, :], hy_r.shape), pltpu.roll(hy_r, 1, 0))
        put_wide(hz_t, y, ht)
        put_wide(f_s, y, wide(ie, y) * ex[r, :] - (hy_r - low) + ht)
        put_wide(g_s, y, -ht)
    for c in range(CHUNKS):
        up_local(yrow, NYL, c, f_s, g_s, cy, w_out, pay)
    pay[2:5] = y_mat[...]


def first_z_kernel(hx, ez, y_even, y_odd, hz, ey, ie, ch, z_mat, cz, pay, w_out, hx_t, f_s, g_s):
    for y in range(NYL):
        r = plain(y)
        up = ez[plain(y + 1), :] if y < NYL - 1 else from_above("gy", y_even[...], y_odd[...])
        ht = hx[r, :] - wide(ch, y) * (up - ez[r, :])
        hz_r = hz[r, :]
        put_wide(hx_t, y, ht)
        put_wide(f_s, y, wide(ie, y) * ey[r, :] - (hz_r - prev_x(hz_r)) + ht)
        put_wide(g_s, y, -ht)
    for c in range(CHUNKS):
        up_local(zrow, NZL, c, f_s, g_s, cz, w_out, pay)
    pay[2:5] = z_mat[...]


def merge_all(axis, top, lower, upper, pay, save, edge):
    stamp, (p, q, inv) = merge_mat((lower[2], lower[3], lower[4]), (upper[2], upper[3], upper[4]))
    (f, g), w = merge_rhs((lower[0], lower[1]), (upper[0], upper[1]), p, q)
    save[0], save[1], save[2], save[3] = p, q, inv, w
    if top is None:
        pay[0], pay[1], pay[2], pay[3], pay[4] = f, g, *stamp
        return
    ga, b, gc = stamp
    share = 1.0 / (ga + b)
    reach = b * share
    high = jnp.broadcast_to(bit_of(axis, top), f.shape) == 1
    pay[0] = jnp.where(high, f, g + reach * f)
    pay[1] = jnp.where(high, ga + b, gc + reach * ga)
    edge[0], edge[1], edge[2] = reach, share, f


def merge_kernel(axis, bit, top, mine, other, pay, save, edge=None):
    side = bit_of(axis, bit)

    @pl.when(side == 0)
    def _():
        merge_all(axis, top, mine, other, pay, save, edge)

    @pl.when(side == 1)
    def _():
        merge_all(axis, top, other, mine, pay, save, edge)


def again_all(axis, top, lower, upper, kept, edge, pay, w_out, f_out):
    (f, g), w = merge_rhs((lower[0], lower[1]), (upper[0], upper[1]), kept[0], kept[1])
    w_out[...] = w
    if top is None:
        pay[0], pay[1] = f, g
        return
    high = jnp.broadcast_to(bit_of(axis, top), f.shape) == 1
    pay[...] = jnp.where(high, f, g + edge[0] * f)
    f_out[...] = f


def again_kernel(axis, bit, mine, other, kept, pay, w_out):
    side = bit_of(axis, bit)

    @pl.when(side == 0)
    def _():
        again_all(axis, None, mine, other, kept, None, pay, w_out, None)

    @pl.when(side == 1)
    def _():
        again_all(axis, None, other, mine, kept, None, pay, w_out, None)


def again_top_kernel(axis, bit, top, mine, other, kept, edge, pay, w_out, f_out):
    side = bit_of(axis, bit)

    @pl.when(side == 0)
    def _():
        again_all(axis, top, mine, other, kept, edge, pay, w_out, f_out)

    @pl.when(side == 1)
    def _():
        again_all(axis, top, other, mine, kept, edge, pay, w_out, f_out)


def ends_of(axis, x_meet, reach, share, f, levels, sources):
    high = jnp.broadcast_to(bit_of(axis, len(levels)), x_meet.shape) == 1
    x_lo = jnp.where(high, x_meet, share * f + reach * x_meet)
    x_hi = jnp.where(high, 0.0, x_meet)
    for bit in reversed(range(len(levels))):
        kept = levels[bit]
        x_mid = kept[0] * x_lo + kept[1] * x_hi + kept[2] * sources[bit]
        upper = jnp.broadcast_to(bit_of(axis, bit), x_lo.shape) == 1
        x_lo, x_hi = jnp.where(upper, x_mid, x_lo), jnp.where(upper, x_hi, x_mid)
    return x_lo, x_hi


def first_ends(axis, mine, other, edge, levels, inv):
    inv[...] = 1.0 / (mine[1] + other[1])
    return ends_of(axis, (mine[0] + other[0]) * inv[...], edge[0], edge[1], edge[2], levels, [s[3] for s in levels])


def down_local(rows, count, c, x_lo, x_hi, coef, w_of, put):
    def get(j, k):
        return coef[j * (count - 1) + k, :, cut(c)]

    def source(k):
        return w_of[k, :, cut(c)]

    tree_down(0, count, x_lo[:, cut(c)], x_hi[:, cut(c)], get, source, put)


def mid_y_kernel(mine, other, edge, s0, s1, cy, w_y, hz_t, hy, hy_u, ex, ie, ch, cz,
                 hz_u, pay, w_out, inv, lo_s, hi_s, f_s, g_s):
    lo_s[...], hi_s[...] = first_ends("gy", mine, other, edge, (s0, s1), inv)
    for c in range(CHUNKS):

        def put(y, x, x_next):
            r = yrow(y, c)
            hz_u[r, :] = hz_t[r, :] + 2.0 * (ch[r, :] * (x_next - x))
            s = hy[plain(y), cut(c)] - hy_u[r, :]
            f_s[r, :] = ie[r, :] * (2.0 * x - ex[plain(y), cut(c)]) + s
            g_s[r, :] = -s

        down_local(yrow, NYL, c, lo_s, hi_s, cy, w_y, put)
        up_local(zrow, NZL, c, f_s, g_s, cz, w_out, pay)


def mid_z_kernel(mine, other, edge, s0, s1, s2, s3, cz, w_z, hx_t, hx, ez1, ez, ie, ch, cy,
                 ey1, hx_u, pay, w_out, inv, lo_s, hi_s, f_s, g_s):
    lo_s[...], hi_s[...] = first_ends("gz", mine, other, edge, (s0, s1, s2, s3), inv)
    for c in range(CHUNKS):

        def put(z, x, x_next):
            r = zrow(z, c)
            ey1[r, :] = x
            hx_u[r, :] = hx_t[r, :] + 2.0 * (ch[r, :] * (x_next - x))

        down_local(zrow, NZL, c, lo_s, hi_s, cz, w_z, put)
        for y in range(NYL):
            r = yrow(y, c)
            n = plain(y)
            s = hx[n, cut(c)] - hx_u[r, :]
            f_s[r, :] = ie[r, :] * (2.0 * ez1[n, cut(c)] - ez[n, cut(c)]) + s
            g_s[r, :] = -s
        up_local(yrow, NYL, c, f_s, g_s, cy, w_out, pay)


def end_kernel(axis, rows, count, steps, *refs):
    mine, other, inv, edge, f = refs[:5]
    levels, sources = refs[5:5 + steps], refs[5 + steps:5 + 2 * steps]
    coef, w_of, h_u, ch, e_new, h_new, done, lo_s, hi_s, e_s, h_s = refs[5 + 2 * steps:]
    done[...] = jnp.zeros_like(done)
    lo_s[...], hi_s[...] = ends_of(axis, (mine[...] + other[...]) * inv[...], edge[0], edge[1], f[...], levels,
                                   [s[...] for s in sources])
    for c in range(CHUNKS):

        def put(i, x, x_next):
            r = rows(i, c)
            e_s[r, :] = x
            h_s[r, :] = h_u[r, :] - ch[r, :] * (x_next - x)

        down_local(rows, count, c, lo_s, hi_s, coef, w_of, put)
        for y in range(NYL):
            e_new[plain(y), cut(c)] = e_s[yrow(y, c), :]
            h_new[plain(y), cut(c)] = h_s[yrow(y, c), :]


def run_row(t):
    return pl.ds(t, 8, stride=RUN)


def x_solve(rhs, ie, ch, cx, keep, x_out, r_t, e_t, h_t, w_s):
    for c in range(CHUNKS):
        r_t[cut(c), :] = rhs[:, cut(c)].T
        if keep:
            e_t[cut(c), :] = tall(ie, c).T
            h_t[cut(c), :] = tall(ch, c).T
    inner = RUN - 1
    merges = inner + 3

    def put_coefs(k, coefs):
        for j in range(3):
            cx[j * merges + k] = coefs[j]

    def get(j, k):
        return cx[j * merges + k]

    def source(k):
        return w_s[k]

    def put_w(k, w):
        w_s[k] = w

    spot = lax.broadcasted_iota(jnp.int32, (8, LANES), 0)
    if keep:
        stamp = tree_mat(0, RUN, lambda t: (e_t[run_row(t), :], h_t[run_row(t), :], None), put_coefs)
        for step in range(3):
            nearby = tuple(pltpu.roll(part, 8 - (1 << step), 0) for part in stamp)
            stamp, coefs = merge_mat(stamp, nearby)
            put_coefs(inner + step, coefs)
        cx[3 * merges] = stamp[0] + stamp[1]
    pair = tree_rhs(0, RUN, lambda t: (r_t[run_row(t), :], jnp.zeros((8, LANES), F32)), get, put_w)
    for step in range(3):
        nearby = tuple(pltpu.roll(part, 8 - (1 << step), 0) for part in pair)
        pair, w = merge_rhs(pair, nearby, get(0, inner + step), get(1, inner + step))
        put_w(inner + step, w)
    x_lo = pair[0] / cx[3 * merges]
    x_hi = jnp.zeros_like(x_lo)
    for step in reversed(range(3)):
        k = inner + step
        x_mid = get(0, k) * x_lo + get(1, k) * x_hi + get(2, k) * source(k)
        upper = ((spot >> step) & 1) == 1
        x_lo, x_hi = (jnp.where(upper, pltpu.roll(x_mid, 1 << step, 0), x_lo),
                      jnp.where(upper, pltpu.roll(x_hi, 1 << step, 0), x_mid))

    def put_x(t, x, x_next):
        r_t[run_row(t), :] = x

    tree_down(0, RUN, x_lo, x_hi, get, source, put_x)
    for c in range(CHUNKS):
        x_out[:, cut(c)] = r_t[cut(c), :].T


def first_x_kernel(hy, ex, z_even, z_odd, hx, y_even, y_odd, ez, ie, ch, ez1, hy_u, cx, r_t, e_t, h_t, w_s, rhs, ex_rim):
    ex_rim[...] = from_above("gz", z_even[...], z_odd[...])
    for y in range(NYL):
        r = plain(y)
        ex_r = ex[r, :]
        z_of = lax.broadcasted_iota(jnp.int32, ex_r.shape, 0)
        up = jnp.where(z_of == NZL - 1, jnp.broadcast_to(ex_rim[y:y + 1, :], ex_r.shape), pltpu.roll(ex_r, NZL - 1, 0))
        ht = hy[r, :] - wide(ch, y) * (up - ex_r)
        low = hx[plain(y - 1), :] if y > 0 else from_below("gy", y_even[...], y_odd[...])
        put_wide(hy_u, y, ht)
        rhs[r, :] = wide(ie, y) * ez[r, :] + (ht - prev_x(ht)) - (hx[r, :] - low)
    x_solve(rhs, ie, ch, cx, True, ez1, r_t, e_t, h_t, w_s)
    for y in range(NYL):
        x = ez1[plain(y), :]
        put_wide(hy_u, y, wide(hy_u, y) + 2.0 * (wide(ch, y) * (next_x(x) - x)))


def last_x_kernel(ey1, ey, hz, hz_u, ie, ch, cx, ey_new, hz_new, done, r_t, w_s, rhs):
    done[...] = jnp.zeros_like(done)
    for y in range(NYL):
        r = plain(y)
        s = hz[r, :] - wide(hz_u, y)
        rhs[r, :] = wide(ie, y) * (2.0 * wide(ey1, y) - ey[r, :]) + (s - prev_x(s))
    x_solve(rhs, ie, ch, cx, False, ey_new, r_t, None, None, w_s)
    for y in range(NYL):
        r = plain(y)
        x = ey_new[r, :]
        hz_new[r, :] = wide(hz_u, y) - wide(ch, y) * (next_x(x) - x)


VM = pl.BlockSpec(memory_space=pltpu.VMEM)


def shape(*dims):
    return jax.ShapeDtypeStruct(dims, F32)


class Order:
    def __init__(self):
        self.last = None

    def __call__(self, kernel, args, outs, scratch=(), specs=None, after=(), name=None):
        after = list(after) + ([] if self.last is None else [self.last])
        count = len(args)

        def body(*refs):
            kernel(*refs[:count], *refs[count + len(after):])

        results = pl.pallas_call(
            body,
            out_shape=[shape(*dims) for dims in outs],
            in_specs=(specs or [VM] * count) + [pl.BlockSpec(memory_space=pl.ANY)] * len(after),
            out_specs=[VM] * len(outs),
            scratch_shapes=[pltpu.VMEM(dims, F32) for dims in scratch],
            compiler_params=pltpu.CompilerParams(vmem_limit_bytes=16 * 1024 * 1024),
            name=name,
        )(*args, *after)
        self.last = results[-1]
        return results


FIELD = (ROWS, NX)
PACKED = (ROWS * CHUNKS, LANES)
Y1, Z1 = (NZL, NX), (NYL, NX)


def on_device(ex, ey, ez, hx, hy, hz, material, eps_table, mu_table):
    ex, ey, ez, hx, hy, hz, material = (a.reshape(FIELD) for a in (ex, ey, ez, hx, hy, hz, material))

    call = Order()

    inputs = (ex, ey, ez, hx, hy, hz, material)
    ex, ey, ez, hx, hy, hz, material, y_even, y_odd, z_even, z_odd, tables = pl.pallas_call(
        inputs_kernel,
        out_shape=[jax.ShapeDtypeStruct(FIELD, a.dtype) for a in inputs]
        + [shape(*Y1), shape(*Y1), shape(*Z1), shape(*Z1), shape(32, LANES)],
        in_specs=[pl.BlockSpec(memory_space=pltpu.HBM)] * 9,
        out_specs=[VM] * 12,
        scratch_shapes=[pltpu.SMEM((16,), F32), pltpu.SMEM((16,), F32), pltpu.SemaphoreType.DMA((9,))],
        compiler_params=pltpu.CompilerParams(vmem_limit_bytes=52 * 1024 * 1024),
        name="inputs",
    )(*inputs, eps_table, mu_table)
    y_even, z_even = met(y_even, "gy", 0), met(z_even, "gz", 0)
    y_odd, z_odd = met(y_odd, "gy", 1), met(z_odd, "gz", 1)

    ie, ch, y_mat, z_mat, cy, cz = call(
        bands_kernel, (material, tables),
        (PACKED, PACKED, (3,) + Y1, (3,) + Z1, (45,) + Y1, (21,) + Z1), name="bands")

    pay_y, w_y, hz_t = call(first_y_kernel, (hz, ey, ex, hy, z_even, z_odd, ie, ch, y_mat, cy),
                            ((5,) + Y1, (15,) + Y1, PACKED), (PACKED, PACKED, Z1), after=(y_even, y_odd), name="first_y")
    pay_z, w_z, hx_t = call(first_z_kernel, (hx, ez, y_even, y_odd, hz, ey, ie, ch, z_mat, cz),
                            ((5,) + Z1, (7,) + Z1, PACKED), (PACKED, PACKED), name="first_z")

    def merge(pay, axis, step, plane, saved, top=None):
        flip, bit = step
        other = swapped(pay, axis, flip)
        kernel = functools.partial(merge_kernel, axis, bit, top)
        if top is None:
            pay, kept = call(kernel, (pay, other), ((5,) + plane, (4,) + plane), name="merge_" + axis)
            saved.append(kept)
            return pay
        pay, kept, edge = call(kernel, (pay, other), ((2,) + plane, (4,) + plane, (3,) + plane), name="merge_" + axis)
        saved.append(kept)
        return pay, edge

    def again(pay, axis, step, plane, kept, sources, top=None, edge=None):
        flip, bit = step
        other = swapped(pay, axis, flip)
        if top is None:
            pay, w = call(functools.partial(again_kernel, axis, bit), (pay, other, kept), ((2,) + plane, plane),
                          name="again_" + axis)
            sources.append(w)
            return pay
        pay, w, f = call(functools.partial(again_top_kernel, axis, bit, top), (pay, other, kept, edge),
                         (plane, plane, plane), name="again_" + axis)
        sources.append(w)
        return pay, f

    save_z, save_y, from_z, from_y = [], [], [], []
    pay_y = merge(pay_y, "gy", Y_STEPS[0], Y1, save_y)
    pay_z = merge(pay_z, "gz", Z_STEPS[0], Z1, save_z)
    ez1, hy_u, cx = call(first_x_kernel, (hy, ex, z_even, z_odd, hx, y_even, y_odd, ez, ie, ch),
                         (FIELD, PACKED, (3 * (RUN + 2) + 1, 8, LANES)),
                         ((NX, LANES), (NX, LANES), (NX, LANES), (RUN + 2, 8, LANES), FIELD, Z1), name="first_x")
    pay_y, edge_y = merge(pay_y, "gy", Y_STEPS[1], Y1, save_y, Y_STEPS[2][1])
    pay_z = merge(pay_z, "gz", Z_STEPS[1], Z1, save_z)
    hz_u, pay_z2, w_z2, inv_y = call(
        mid_y_kernel, (pay_y, swapped(pay_y, "gy", Y_STEPS[2][0]), edge_y, *save_y, cy, w_y, hz_t, hy, hy_u, ex, ie, ch, cz),
        (PACKED, (2,) + Z1, (7,) + Z1, Y1), (Y1, Y1, PACKED, PACKED), name="mid_y")
    pay_z = merge(pay_z, "gz", Z_STEPS[2], Z1, save_z)
    pay_z2 = again(pay_z2, "gz", Z_STEPS[0], Z1, save_z[0], from_z)
    pay_z, edge_z = merge(pay_z, "gz", Z_STEPS[3], Z1, save_z, Z_STEPS[4][1])
    pay_z2 = again(pay_z2, "gz", Z_STEPS[1], Z1, save_z[1], from_z)
    ey1, hx_u, pay_y2, w_y2, inv_z = call(
        mid_z_kernel, (pay_z, swapped(pay_z, "gz", Z_STEPS[4][0]), edge_z, *save_z, cz, w_z, hx_t, hx, ez1, ez, ie, ch, cy),
        (PACKED, PACKED, (2,) + Y1, (15,) + Y1, Z1), (Z1, Z1, PACKED, PACKED), name="mid_z")
    pay_y2 = again(pay_y2, "gy", Y_STEPS[0], Y1, save_y[0], from_y)
    pay_z2 = again(pay_z2, "gz", Z_STEPS[2], Z1, save_z[2], from_z)
    pay_z2, f_z = again(pay_z2, "gz", Z_STEPS[3], Z1, save_z[3], from_z, Z_STEPS[4][1], edge_z)
    pay_y2, f_y = again(pay_y2, "gy", Y_STEPS[1], Y1, save_y[1], from_y, Y_STEPS[2][1], edge_y)
    mark = (8, LANES)
    ey_new, hz_new, _ = call(last_x_kernel, (ey1, ey, hz, hz_u, ie, ch, cx), (FIELD, FIELD, mark),
                             ((NX, LANES), (RUN + 2, 8, LANES), FIELD), name="last_x")
    ex_new, hy_new, _ = call(
        functools.partial(end_kernel, "gz", zrow, NZL, 4),
        (pay_z2, swapped(pay_z2, "gz", Z_STEPS[4][0]), inv_z, edge_z, f_z, *save_z, *from_z, cz, w_z2, hy_u, ch),
        (FIELD, FIELD, mark), (Z1, Z1, PACKED, PACKED), name="end_z")
    ez_new, hx_new, _ = call(
        functools.partial(end_kernel, "gy", yrow, NYL, 2),
        (pay_y2, swapped(pay_y2, "gy", Y_STEPS[2][0]), inv_y, edge_y, f_y, *save_y, *from_y, cy, w_y2, hx_u, ch),
        (FIELD, FIELD, mark), (Y1, Y1, PACKED, PACKED), name="end_y")

    return tuple(a.reshape(NYL, NZL, NX) for a in (ex_new, ey_new, ez_new, hx_new, hy_new, hz_new))


def solution(mesh):
    cells = P("gy", "gz", None)
    return jax.shard_map(
        on_device,
        mesh=mesh,
        in_specs=(cells,) * 7 + (P(), P()),
        out_specs=(cells,) * 6,
        check_vma=False,
    )
```

```python
import functools

import jax
import jax.numpy as jnp
from jax import lax
from jax.experimental import pallas as pl
from jax.experimental.pallas import tpu as pltpu
from jax.sharding import PartitionSpec as P

courant = 16.0
F32 = jnp.float32
NYL, NZL, NX = 16, 8, 512
ROWS = NYL * NZL
LANES = 128
CHUNKS = NX // LANES
RUN = NX // 8

Y_STEPS = ((1, 0), (2, 1), (6, 2))
Z_STEPS = ((1, 0), (2, 1), (6, 2), (8, 3), (24, 4))


def met(array, axis, first):
    size = lax.axis_size(axis)
    low = range(first, size - 1, 2)
    return lax.ppermute(array, axis, [(i, i + 1) for i in low] + [(i + 1, i) for i in low])


def swapped(array, axis, flip):
    size = lax.axis_size(axis)
    return lax.ppermute(array, axis, [(i, i ^ flip) for i in range(size)])


def merge_mat(s1, s2):
    ga1, b1, gc1 = s1
    ga2, b2, gc2 = s2
    ground = ga2 if gc1 is None else gc1 + ga2
    inv = 1.0 / (b1 + b2 + ground)
    p, q = b1 * inv, b2 * inv
    right = q * ground
    return (ga1 + p * ground, p * b2, right if gc2 is None else gc2 + right), (p, q, inv)


def merge_rhs(r1, r2, p, q):
    w = r1[1] + r2[0]
    return (r1[0] + p * w, r2[1] + q * w), w


def tree_mat(lo, hi, leaf, put):
    if hi - lo == 1:
        return leaf(lo)
    mid = (lo + hi) // 2
    left = tree_mat(lo, mid, leaf, put)
    right = tree_mat(mid, hi, leaf, put)
    stamp, coefs = merge_mat(left, right)
    put(mid - 1, coefs)
    return stamp


def tree_rhs(lo, hi, leaf, coef, put):
    if hi - lo == 1:
        return leaf(lo)
    mid = (lo + hi) // 2
    left = tree_rhs(lo, mid, leaf, coef, put)
    right = tree_rhs(mid, hi, leaf, coef, put)
    out, w = merge_rhs(left, right, coef(0, mid - 1), coef(1, mid - 1))
    put(mid - 1, w)
    return out


def tree_down(lo, hi, x_lo, x_hi, coef, source, put):
    if hi - lo == 1:
        put(lo, x_lo, x_hi)
        return
    mid = (lo + hi) // 2
    k = mid - 1
    x_mid = coef(0, k) * x_lo + coef(1, k) * x_hi + coef(2, k) * source(k)
    tree_down(lo, mid, x_lo, x_mid, coef, source, put)
    tree_down(mid, hi, x_mid, x_hi, coef, source, put)


def cut(c):
    return pl.ds(c * LANES, LANES)


def plain(y):
    return pl.ds(y * NZL, NZL)


def yrow(y, c):
    return pl.ds((y * CHUNKS + c) * NZL, NZL)


def zrow(z, c):
    return pl.ds(c * NZL + z, NYL, stride=CHUNKS * NZL)


def wide(ref, y):
    return jnp.concatenate([ref[yrow(y, c), :] for c in range(CHUNKS)], axis=1)


def put_wide(ref, y, value):
    for c in range(CHUNKS):
        ref[yrow(y, c), :] = value[:, c * LANES:(c + 1) * LANES]


def tall(ref, c):
    return jnp.concatenate([ref[yrow(y, c), :] for y in range(NYL)], axis=0)


def next_x(v):
    lane = lax.broadcasted_iota(jnp.int32, v.shape, 1)
    return jnp.where(lane == NX - 1, 0.0, pltpu.roll(v, NX - 1, 1))


def prev_x(v):
    lane = lax.broadcasted_iota(jnp.int32, v.shape, 1)
    return jnp.where(lane == 0, 0.0, pltpu.roll(v, 1, 1))


def bit_of(axis, bit):
    return (lax.axis_index(axis) >> bit) & 1


def inputs_kernel(*refs):
    away, here = refs[:7], refs[7:14]
    y_even, y_odd, z_even, z_odd, sems = refs[14:]
    copies = [pltpu.make_async_copy(away[i], here[i], sems.at[i]) for i in range(7)]
    for copy in copies:
        copy.start()
    for copy in copies:
        copy.wait()
    ex, ez, hx, hy = here[0], here[2], here[3], here[4]

    def fill(axis, low, high, even, odd):
        up = (lax.axis_index(axis) & 1) == 0

        @pl.when(up)
        def _():
            low(even)
            high(odd)

        @pl.when(jnp.logical_not(up))
        def _():
            high(even)
            low(odd)

    def hx_last(out):
        out[...] = hx[plain(NYL - 1), :]

    def ez_first(out):
        out[...] = ez[plain(0), :]

    def hy_last(out):
        for y in range(NYL):
            out[y:y + 1, :] = hy[(y + 1) * NZL - 1:(y + 1) * NZL, :]

    def ex_first(out):
        for y in range(NYL):
            out[y:y + 1, :] = ex[y * NZL:y * NZL + 1, :]

    fill("gy", hx_last, ez_first, y_even, y_odd)
    fill("gz", hy_last, ex_first, z_even, z_odd)


def from_below(axis, even, odd):
    return jnp.where(jnp.broadcast_to(lax.axis_index(axis) & 1, even.shape) == 1, even, odd)


def from_above(axis, even, odd):
    return jnp.where(jnp.broadcast_to(lax.axis_index(axis) & 1, even.shape) == 0, even, odd)


def bands_kernel(material, eps, mu, ie, ch, y_mat, z_mat, cy, cz):
    spread = [jnp.full((NZL, LANES), table[k], F32) for table in (eps, mu) for k in range(16)]
    for y in range(NYL):
        for c in range(CHUNKS):
            label = material[plain(y), cut(c)]
            e_val, m_val = spread[0], spread[16]
            for k in range(1, 16):
                hit = label == k
                e_val = jnp.where(hit, spread[k], e_val)
                m_val = jnp.where(hit, spread[16 + k], m_val)
            ie[yrow(y, c), :] = e_val * (1.0 / courant)
            ch[yrow(y, c), :] = courant / m_val
    for c in range(CHUNKS):
        for rows, count, mat, coef in ((yrow, NYL, y_mat, cy), (zrow, NZL, z_mat, cz)):

            def leaf(i):
                return ie[rows(i, c), :], ch[rows(i, c), :], None

            def put(k, coefs):
                for j in range(3):
                    coef[j * (count - 1) + k, :, cut(c)] = coefs[j]

            for j, part in enumerate(tree_mat(0, count, leaf, put)):
                mat[j, :, cut(c)] = part


def up_local(rows, count, c, f_of, g_of, coef, w_out, pay):
    def leaf(i):
        return f_of[rows(i, c), :], g_of[rows(i, c), :]

    def get(j, k):
        return coef[j * (count - 1) + k, :, cut(c)]

    def put(k, w):
        w_out[k, :, cut(c)] = w

    f, g = tree_rhs(0, count, leaf, get, put)
    pay[0, :, cut(c)] = f
    pay[1, :, cut(c)] = g


def first_y_kernel(hz, ey, ex, hy, z_even, z_odd, ie, ch, y_mat, cy, pay, w_out, hz_t, f_s, g_s, hy_rim):
    hy_rim[...] = from_below("gz", z_even[...], z_odd[...])
    for y in range(NYL):
        r = plain(y)
        ey_r = ey[r, :]
        ht = hz[r, :] - wide(ch, y) * (next_x(ey_r) - ey_r)
        hy_r = hy[r, :]
        z_of = lax.broadcasted_iota(jnp.int32, hy_r.shape, 0)
        low = jnp.where(z_of == 0, jnp.broadcast_to(hy_rim[y:y + 1, :], hy_r.shape), pltpu.roll(hy_r, 1, 0))
        put_wide(hz_t, y, ht)
        put_wide(f_s, y, wide(ie, y) * ex[r, :] - (hy_r - low) + ht)
        put_wide(g_s, y, -ht)
    for c in range(CHUNKS):
        up_local(yrow, NYL, c, f_s, g_s, cy, w_out, pay)
    pay[2:5] = y_mat[...]


def first_z_kernel(hx, ez, y_even, y_odd, hz, ey, ie, ch, z_mat, cz, pay, w_out, hx_t, f_s, g_s):
    for y in range(NYL):
        r = plain(y)
        up = ez[plain(y + 1), :] if y < NYL - 1 else from_above("gy", y_even[...], y_odd[...])
        ht = hx[r, :] - wide(ch, y) * (up - ez[r, :])
        hz_r = hz[r, :]
        put_wide(hx_t, y, ht)
        put_wide(f_s, y, wide(ie, y) * ey[r, :] - (hz_r - prev_x(hz_r)) + ht)
        put_wide(g_s, y, -ht)
    for c in range(CHUNKS):
        up_local(zrow, NZL, c, f_s, g_s, cz, w_out, pay)
    pay[2:5] = z_mat[...]


def merge_all(axis, top, lower, upper, pay, save, edge):
    stamp, (p, q, inv) = merge_mat((lower[2], lower[3], lower[4]), (upper[2], upper[3], upper[4]))
    (f, g), w = merge_rhs((lower[0], lower[1]), (upper[0], upper[1]), p, q)
    save[0], save[1], save[2], save[3] = p, q, inv, w
    if top is None:
        pay[0], pay[1], pay[2], pay[3], pay[4] = f, g, *stamp
        return
    ga, b, gc = stamp
    share = 1.0 / (ga + b)
    reach = b * share
    high = jnp.broadcast_to(bit_of(axis, top), f.shape) == 1
    pay[0] = jnp.where(high, f, g + reach * f)
    pay[1] = jnp.where(high, ga + b, gc + reach * ga)
    edge[0], edge[1], edge[2] = reach, share, f


def merge_kernel(axis, bit, top, mine, other, pay, save, edge=None):
    side = bit_of(axis, bit)

    @pl.when(side == 0)
    def _():
        merge_all(axis, top, mine, other, pay, save, edge)

    @pl.when(side == 1)
    def _():
        merge_all(axis, top, other, mine, pay, save, edge)


def again_all(axis, top, lower, upper, kept, edge, pay, w_out, f_out):
    (f, g), w = merge_rhs((lower[0], lower[1]), (upper[0], upper[1]), kept[0], kept[1])
    w_out[...] = w
    if top is None:
        pay[0], pay[1] = f, g
        return
    high = jnp.broadcast_to(bit_of(axis, top), f.shape) == 1
    pay[...] = jnp.where(high, f, g + edge[0] * f)
    f_out[...] = f


def again_kernel(axis, bit, mine, other, kept, pay, w_out):
    side = bit_of(axis, bit)

    @pl.when(side == 0)
    def _():
        again_all(axis, None, mine, other, kept, None, pay, w_out, None)

    @pl.when(side == 1)
    def _():
        again_all(axis, None, other, mine, kept, None, pay, w_out, None)


def again_top_kernel(axis, bit, top, mine, other, kept, edge, pay, w_out, f_out):
    side = bit_of(axis, bit)

    @pl.when(side == 0)
    def _():
        again_all(axis, top, mine, other, kept, edge, pay, w_out, f_out)

    @pl.when(side == 1)
    def _():
        again_all(axis, top, other, mine, kept, edge, pay, w_out, f_out)


def ends_of(axis, x_meet, reach, share, f, levels, sources):
    high = jnp.broadcast_to(bit_of(axis, len(levels)), x_meet.shape) == 1
    x_lo = jnp.where(high, x_meet, share * f + reach * x_meet)
    x_hi = jnp.where(high, 0.0, x_meet)
    for bit in reversed(range(len(levels))):
        kept = levels[bit]
        x_mid = kept[0] * x_lo + kept[1] * x_hi + kept[2] * sources[bit]
        upper = jnp.broadcast_to(bit_of(axis, bit), x_lo.shape) == 1
        x_lo, x_hi = jnp.where(upper, x_mid, x_lo), jnp.where(upper, x_hi, x_mid)
    return x_lo, x_hi


def first_ends(axis, mine, other, edge, levels, inv):
    inv[...] = 1.0 / (mine[1] + other[1])
    return ends_of(axis, (mine[0] + other[0]) * inv[...], edge[0], edge[1], edge[2], levels, [s[3] for s in levels])


def down_local(rows, count, c, x_lo, x_hi, coef, w_of, put):
    def get(j, k):
        return coef[j * (count - 1) + k, :, cut(c)]

    def source(k):
        return w_of[k, :, cut(c)]

    tree_down(0, count, x_lo[:, cut(c)], x_hi[:, cut(c)], get, source, put)


def mid_y_kernel(mine, other, edge, s0, s1, cy, w_y, hz_t, hy, hy_u, ex, ie, ch, cz,
                 hz_u, pay, w_out, inv, lo_s, hi_s, f_s, g_s):
    lo_s[...], hi_s[...] = first_ends("gy", mine, other, edge, (s0, s1), inv)
    for c in range(CHUNKS):

        def put(y, x, x_next):
            r = yrow(y, c)
            hz_u[r, :] = hz_t[r, :] + 2.0 * (ch[r, :] * (x_next - x))
            s = hy[plain(y), cut(c)] - hy_u[r, :]
            f_s[r, :] = ie[r, :] * (2.0 * x - ex[plain(y), cut(c)]) + s
            g_s[r, :] = -s

        down_local(yrow, NYL, c, lo_s, hi_s, cy, w_y, put)
        up_local(zrow, NZL, c, f_s, g_s, cz, w_out, pay)


def mid_z_kernel(mine, other, edge, s0, s1, s2, s3, cz, w_z, hx_t, hx, ez1, ez, ie, ch, cy,
                 ey1, hx_u, pay, w_out, inv, lo_s, hi_s, f_s, g_s):
    lo_s[...], hi_s[...] = first_ends("gz", mine, other, edge, (s0, s1, s2, s3), inv)
    for c in range(CHUNKS):

        def put(z, x, x_next):
            r = zrow(z, c)
            ey1[r, :] = x
            hx_u[r, :] = hx_t[r, :] + 2.0 * (ch[r, :] * (x_next - x))

        down_local(zrow, NZL, c, lo_s, hi_s, cz, w_z, put)
        for y in range(NYL):
            r = yrow(y, c)
            n = plain(y)
            s = hx[n, cut(c)] - hx_u[r, :]
            f_s[r, :] = ie[r, :] * (2.0 * ez1[n, cut(c)] - ez[n, cut(c)]) + s
            g_s[r, :] = -s
        up_local(yrow, NYL, c, f_s, g_s, cy, w_out, pay)


def end_kernel(axis, rows, count, steps, *refs):
    mine, other, inv, edge, f = refs[:5]
    levels, sources = refs[5:5 + steps], refs[5 + steps:5 + 2 * steps]
    coef, w_of, h_u, ch, e_new, h_new, done, lo_s, hi_s, e_s, h_s = refs[5 + 2 * steps:]
    done[...] = jnp.zeros_like(done)
    lo_s[...], hi_s[...] = ends_of(axis, (mine[...] + other[...]) * inv[...], edge[0], edge[1], f[...], levels,
                                   [s[...] for s in sources])
    for c in range(CHUNKS):

        def put(i, x, x_next):
            r = rows(i, c)
            e_s[r, :] = x
            h_s[r, :] = h_u[r, :] - ch[r, :] * (x_next - x)

        down_local(rows, count, c, lo_s, hi_s, coef, w_of, put)
        for y in range(NYL):
            e_new[plain(y), cut(c)] = e_s[yrow(y, c), :]
            h_new[plain(y), cut(c)] = h_s[yrow(y, c), :]


def run_row(t):
    return pl.ds(t, 8, stride=RUN)


def x_solve(rhs, ie, ch, cx, keep, x_out, r_t, e_t, h_t, w_s):
    for c in range(CHUNKS):
        r_t[cut(c), :] = rhs[:, cut(c)].T
        if keep:
            e_t[cut(c), :] = tall(ie, c).T
            h_t[cut(c), :] = tall(ch, c).T
    inner = RUN - 1
    merges = inner + 3

    def put_coefs(k, coefs):
        for j in range(3):
            cx[j * merges + k] = coefs[j]

    def get(j, k):
        return cx[j * merges + k]

    def source(k):
        return w_s[k]

    def put_w(k, w):
        w_s[k] = w

    spot = lax.broadcasted_iota(jnp.int32, (8, LANES), 0)
    if keep:
        stamp = tree_mat(0, RUN, lambda t: (e_t[run_row(t), :], h_t[run_row(t), :], None), put_coefs)
        for step in range(3):
            nearby = tuple(pltpu.roll(part, 8 - (1 << step), 0) for part in stamp)
            stamp, coefs = merge_mat(stamp, nearby)
            put_coefs(inner + step, coefs)
        cx[3 * merges] = stamp[0] + stamp[1]
    pair = tree_rhs(0, RUN, lambda t: (r_t[run_row(t), :], jnp.zeros((8, LANES), F32)), get, put_w)
    for step in range(3):
        nearby = tuple(pltpu.roll(part, 8 - (1 << step), 0) for part in pair)
        pair, w = merge_rhs(pair, nearby, get(0, inner + step), get(1, inner + step))
        put_w(inner + step, w)
    x_lo = pair[0] / cx[3 * merges]
    x_hi = jnp.zeros_like(x_lo)
    for step in reversed(range(3)):
        k = inner + step
        x_mid = get(0, k) * x_lo + get(1, k) * x_hi + get(2, k) * source(k)
        upper = ((spot >> step) & 1) == 1
        x_lo, x_hi = (jnp.where(upper, pltpu.roll(x_mid, 1 << step, 0), x_lo),
                      jnp.where(upper, pltpu.roll(x_hi, 1 << step, 0), x_mid))

    def put_x(t, x, x_next):
        r_t[run_row(t), :] = x

    tree_down(0, RUN, x_lo, x_hi, get, source, put_x)
    for c in range(CHUNKS):
        x_out[:, cut(c)] = r_t[cut(c), :].T


def first_x_kernel(hy, ex, z_even, z_odd, hx, y_even, y_odd, ez, ie, ch, ez1, hy_u, cx, r_t, e_t, h_t, w_s, rhs, ex_rim):
    ex_rim[...] = from_above("gz", z_even[...], z_odd[...])
    for y in range(NYL):
        r = plain(y)
        ex_r = ex[r, :]
        z_of = lax.broadcasted_iota(jnp.int32, ex_r.shape, 0)
        up = jnp.where(z_of == NZL - 1, jnp.broadcast_to(ex_rim[y:y + 1, :], ex_r.shape), pltpu.roll(ex_r, NZL - 1, 0))
        ht = hy[r, :] - wide(ch, y) * (up - ex_r)
        low = hx[plain(y - 1), :] if y > 0 else from_below("gy", y_even[...], y_odd[...])
        put_wide(hy_u, y, ht)
        rhs[r, :] = wide(ie, y) * ez[r, :] + (ht - prev_x(ht)) - (hx[r, :] - low)
    x_solve(rhs, ie, ch, cx, True, ez1, r_t, e_t, h_t, w_s)
    for y in range(NYL):
        x = ez1[plain(y), :]
        put_wide(hy_u, y, wide(hy_u, y) + 2.0 * (wide(ch, y) * (next_x(x) - x)))


def last_x_kernel(ey1, ey, hz, hz_u, ie, ch, cx, ey_new, hz_new, done, r_t, w_s, rhs):
    done[...] = jnp.zeros_like(done)
    for y in range(NYL):
        r = plain(y)
        s = hz[r, :] - wide(hz_u, y)
        rhs[r, :] = wide(ie, y) * (2.0 * wide(ey1, y) - ey[r, :]) + (s - prev_x(s))
    x_solve(rhs, ie, ch, cx, False, ey_new, r_t, None, None, w_s)
    for y in range(NYL):
        r = plain(y)
        x = ey_new[r, :]
        hz_new[r, :] = wide(hz_u, y) - wide(ch, y) * (next_x(x) - x)


VM = pl.BlockSpec(memory_space=pltpu.VMEM)


def shape(*dims):
    return jax.ShapeDtypeStruct(dims, F32)


class Order:
    def __init__(self):
        self.last = None

    def __call__(self, kernel, args, outs, scratch=(), specs=None, after=(), name=None):
        after = list(after) + ([] if self.last is None else [self.last])
        count = len(args)

        def body(*refs):
            kernel(*refs[:count], *refs[count + len(after):])

        results = pl.pallas_call(
            body,
            out_shape=[shape(*dims) for dims in outs],
            in_specs=(specs or [VM] * count) + [pl.BlockSpec(memory_space=pl.ANY)] * len(after),
            out_specs=[VM] * len(outs),
            scratch_shapes=[pltpu.VMEM(dims, F32) for dims in scratch],
            compiler_params=pltpu.CompilerParams(vmem_limit_bytes=16 * 1024 * 1024),
            name=name,
        )(*args, *after)
        self.last = results[-1]
        return results


FIELD = (ROWS, NX)
PACKED = (ROWS * CHUNKS, LANES)
Y1, Z1 = (NZL, NX), (NYL, NX)


def on_device(ex, ey, ez, hx, hy, hz, material, eps_table, mu_table):
    ex, ey, ez, hx, hy, hz, material = (a.reshape(FIELD) for a in (ex, ey, ez, hx, hy, hz, material))

    call = Order()

    inputs = (ex, ey, ez, hx, hy, hz, material)
    ex, ey, ez, hx, hy, hz, material, y_even, y_odd, z_even, z_odd = pl.pallas_call(
        inputs_kernel,
        out_shape=[jax.ShapeDtypeStruct(FIELD, a.dtype) for a in inputs]
        + [shape(*Y1), shape(*Y1), shape(*Z1), shape(*Z1)],
        in_specs=[pl.BlockSpec(memory_space=pltpu.HBM)] * 7,
        out_specs=[VM] * 11,
        scratch_shapes=[pltpu.SemaphoreType.DMA((7,))],
        compiler_params=pltpu.CompilerParams(vmem_limit_bytes=52 * 1024 * 1024),
        name="inputs",
    )(*inputs)
    y_even, z_even = met(y_even, "gy", 0), met(z_even, "gz", 0)
    y_odd, z_odd = met(y_odd, "gy", 1), met(z_odd, "gz", 1)

    ie, ch, y_mat, z_mat, cy, cz = call(
        bands_kernel, (material, eps_table, mu_table),
        (PACKED, PACKED, (3,) + Y1, (3,) + Z1, (45,) + Y1, (21,) + Z1),
        specs=[VM] + [pl.BlockSpec(memory_space=pltpu.SMEM)] * 2, name="bands")

    pay_y, w_y, hz_t = call(first_y_kernel, (hz, ey, ex, hy, z_even, z_odd, ie, ch, y_mat, cy),
                            ((5,) + Y1, (15,) + Y1, PACKED), (PACKED, PACKED, Z1), after=(y_even, y_odd), name="first_y")
    pay_z, w_z, hx_t = call(first_z_kernel, (hx, ez, y_even, y_odd, hz, ey, ie, ch, z_mat, cz),
                            ((5,) + Z1, (7,) + Z1, PACKED), (PACKED, PACKED), name="first_z")

    def merge(pay, axis, step, plane, saved, top=None):
        flip, bit = step
        other = swapped(pay, axis, flip)
        kernel = functools.partial(merge_kernel, axis, bit, top)
        if top is None:
            pay, kept = call(kernel, (pay, other), ((5,) + plane, (4,) + plane), name="merge_" + axis)
            saved.append(kept)
            return pay
        pay, kept, edge = call(kernel, (pay, other), ((2,) + plane, (4,) + plane, (3,) + plane), name="merge_" + axis)
        saved.append(kept)
        return pay, edge

    def again(pay, axis, step, plane, kept, sources, top=None, edge=None):
        flip, bit = step
        other = swapped(pay, axis, flip)
        if top is None:
            pay, w = call(functools.partial(again_kernel, axis, bit), (pay, other, kept), ((2,) + plane, plane),
                          name="again_" + axis)
            sources.append(w)
            return pay
        pay, w, f = call(functools.partial(again_top_kernel, axis, bit, top), (pay, other, kept, edge),
                         (plane, plane, plane), name="again_" + axis)
        sources.append(w)
        return pay, f

    save_z, save_y, from_z, from_y = [], [], [], []
    pay_y = merge(pay_y, "gy", Y_STEPS[0], Y1, save_y)
    pay_z = merge(pay_z, "gz", Z_STEPS[0], Z1, save_z)
    ez1, hy_u, cx = call(first_x_kernel, (hy, ex, z_even, z_odd, hx, y_even, y_odd, ez, ie, ch),
                         (FIELD, PACKED, (3 * (RUN + 2) + 1, 8, LANES)),
                         ((NX, LANES), (NX, LANES), (NX, LANES), (RUN + 2, 8, LANES), FIELD, Z1), name="first_x")
    pay_y, edge_y = merge(pay_y, "gy", Y_STEPS[1], Y1, save_y, Y_STEPS[2][1])
    pay_z = merge(pay_z, "gz", Z_STEPS[1], Z1, save_z)
    hz_u, pay_z2, w_z2, inv_y = call(
        mid_y_kernel, (pay_y, swapped(pay_y, "gy", Y_STEPS[2][0]), edge_y, *save_y, cy, w_y, hz_t, hy, hy_u, ex, ie, ch, cz),
        (PACKED, (2,) + Z1, (7,) + Z1, Y1), (Y1, Y1, PACKED, PACKED), name="mid_y")
    pay_z = merge(pay_z, "gz", Z_STEPS[2], Z1, save_z)
    pay_z2 = again(pay_z2, "gz", Z_STEPS[0], Z1, save_z[0], from_z)
    pay_z, edge_z = merge(pay_z, "gz", Z_STEPS[3], Z1, save_z, Z_STEPS[4][1])
    pay_z2 = again(pay_z2, "gz", Z_STEPS[1], Z1, save_z[1], from_z)
    ey1, hx_u, pay_y2, w_y2, inv_z = call(
        mid_z_kernel, (pay_z, swapped(pay_z, "gz", Z_STEPS[4][0]), edge_z, *save_z, cz, w_z, hx_t, hx, ez1, ez, ie, ch, cy),
        (PACKED, PACKED, (2,) + Y1, (15,) + Y1, Z1), (Z1, Z1, PACKED, PACKED), name="mid_z")
    pay_y2 = again(pay_y2, "gy", Y_STEPS[0], Y1, save_y[0], from_y)
    pay_z2 = again(pay_z2, "gz", Z_STEPS[2], Z1, save_z[2], from_z)
    pay_z2, f_z = again(pay_z2, "gz", Z_STEPS[3], Z1, save_z[3], from_z, Z_STEPS[4][1], edge_z)
    pay_y2, f_y = again(pay_y2, "gy", Y_STEPS[1], Y1, save_y[1], from_y, Y_STEPS[2][1], edge_y)
    mark = (8, LANES)
    ey_new, hz_new, _ = call(last_x_kernel, (ey1, ey, hz, hz_u, ie, ch, cx), (FIELD, FIELD, mark),
                             ((NX, LANES), (RUN + 2, 8, LANES), FIELD), name="last_x")
    ex_new, hy_new, _ = call(
        functools.partial(end_kernel, "gz", zrow, NZL, 4),
        (pay_z2, swapped(pay_z2, "gz", Z_STEPS[4][0]), inv_z, edge_z, f_z, *save_z, *from_z, cz, w_z2, hy_u, ch),
        (FIELD, FIELD, mark), (Z1, Z1, PACKED, PACKED), name="end_z")
    ez_new, hx_new, _ = call(
        functools.partial(end_kernel, "gy", yrow, NYL, 2),
        (pay_y2, swapped(pay_y2, "gy", Y_STEPS[2][0]), inv_y, edge_y, f_y, *save_y, *from_y, cy, w_y2, hx_u, ch),
        (FIELD, FIELD, mark), (Y1, Y1, PACKED, PACKED), name="end_y")

    return tuple(a.reshape(NYL, NZL, NX) for a in (ex_new, ey_new, ez_new, hx_new, hy_new, hz_new))


def solution(mesh):
    cells = P("gy", "gz", None)
    return jax.shard_map(
        on_device,
        mesh=mesh,
        in_specs=(cells,) * 7 + (P(), P()),
        out_specs=(cells,) * 6,
        check_vma=False,
    )
```
